128 devices in a mesh: row: 8 (over y, core), col: 16 (over z, x).
Axes of the slice: x: 4, y: 4, z: 4, core: 2. Of those that a mesh axis runs over, the one named last changes fastest.
Arguments:
- amplitudes: float32 [16384, 4096], P('row', 'col'), may hold values from -6 to 6
- integrals: float32 [4096, 16384], P('row', 'col'), may hold values from -0.09375 to 0.09375
- amp_mask: int32 [256, 64], P('row', 'col'), may hold values 0 or 1
- int_mask: int32 [64, 256], P('row', 'col'), may hold values 0 or 1
- occ_shift: float32 [16384], P('row'), may hold values from 0.5 to 4
- virt_shift: float32 [16384], P('col'), may hold values from 0.5 to 4
Outputs:
- update: float32 [16384, 16384], P(None, ('col', 'row'))
The draws below stay inside these ranges and needn't reach their ends.
All inputs are finite; a program needn't handle non-finite values. No bound on the sum of `amp_mask` or of `int_mask` on one device may be relied on, other than what follows from the above.
Results may differ from the reference program's by a relative error of at most 0.00007.
Values sent between devices are 32-bit elements; how exact they have to be, the bound alone decides.
A program may use at most 192 MiB of HBM per device.

```python
import math
import jax
import jax.numpy as jnp
from jax import lax

TILE = 64
K = 4096
P_SIZE = 16384
Q = 16384


def place_ends(drawn, rng, low, top_value):
    dims = drawn.shape
    spot = [jax.random.randint(jax.random.fold_in(rng, axis), (), 0, dims[axis]) for axis in range(len(dims))]
    drawn = drawn.at[tuple(spot)].set(low)
    longest = dims.index(max(dims))
    spot[longest] = (spot[longest] + 1) % dims[longest]
    return drawn.at[tuple(spot)].set(top_value)


def levels(own_key, extent, cuts, smallest, largest):
    gain = 1.0
    for axis_at, blocks in cuts:
        draws = jax.random.uniform(jax.random.fold_in(jax.random.fold_in(own_key, 6), axis_at), (blocks,), jnp.float32, smallest / len(cuts), largest / len(cuts))
        gain = gain * jnp.repeat(jnp.exp(draws), extent[axis_at] // blocks).reshape((-1,) + (1,) * (len(extent) - 1 - axis_at))
    return gain


def normal_values(rng, shape, spread, most, cuts=(), kind=jnp.bfloat16):
    level = levels(rng, shape, cuts, -0.22, 0.18) if cuts else 1.0
    entries = jax.random.normal(rng, shape, jnp.float32) * spread * level
    return jnp.minimum(jnp.maximum(entries, -most), most).astype(kind)


def setup_inputs(seed: int = 0) -> dict:
    key_list = jax.random.split(jax.random.key(seed), 7)
    amplitudes = normal_values(key_list[0], (P_SIZE, K), 1.0, 6.0, ((0, 8), (1, 16)), jnp.float32)
    integrals = normal_values(key_list[1], (K, Q), K ** -0.5, 0.09375, ((0, 8), (1, 16)), jnp.float32)
    amp_mask = place_ends((jax.random.randint(key_list[2], (P_SIZE // TILE, K // TILE), 0, 5) < 3).astype(jnp.int32), jax.random.fold_in(key_list[2], 1), 0, 1)
    int_mask = place_ends((jax.random.randint(key_list[3], (K // TILE, Q // TILE), 0, 5) < 3).astype(jnp.int32), jax.random.fold_in(key_list[3], 1), 0, 1)
    occ_shift = jnp.clip(jnp.exp(math.log(4.0) - 2.0794415 * jax.random.uniform(key_list[4], (P_SIZE,), jnp.float32) ** levels(key_list[4], (P_SIZE,), ((0, 8),), -0.2, 0.2)), 0.5, 4.0)
    virt_shift = jnp.clip(jnp.exp(math.log(4.0) - 2.0794415 * jax.random.uniform(key_list[5], (Q,), jnp.float32) ** levels(key_list[5], (Q,), ((0, 16),), -0.2, 0.2)), 0.5, 4.0)
    return dict(amplitudes=amplitudes, integrals=integrals, amp_mask=amp_mask, int_mask=int_mask, occ_shift=occ_shift, virt_shift=virt_shift)


def apply_mask(block, mask):
    rows, cols = block.shape
    tiled = block.reshape(rows // TILE, TILE, cols // TILE, TILE)
    tiled = tiled * mask.astype(jnp.float32)[:, None, :, None]
    return tiled.reshape(rows, cols)


def reference(amplitudes, integrals, amp_mask, int_mask, occ_shift, virt_shift):
    masked_amps = apply_mask(amplitudes, amp_mask)
    masked_ints = apply_mask(integrals, int_mask)
    ladder = jnp.dot(masked_amps, masked_ints, precision=lax.Precision.HIGHEST, preferred_element_type=jnp.float32)
    return ladder / (occ_shift[:, None] + virt_shift[None, :])
```

```python
import functools

import jax
import jax.numpy as jnp
from jax import lax
from jax.experimental import pallas as pl
from jax.experimental.pallas import tpu as pltpu
from jax.sharding import PartitionSpec as P

MESH = pl.DeviceIdType.MESH
F32, BF16 = jnp.float32, jnp.bfloat16
TILE = 64
ROWS, DEPTH, COLS = 2048, 4096, 1024
CHUNK = 128
CHUNKS = ROWS // CHUNK
HALF = CHUNK // 2
PIECE = 64
PIECES = 512 // PIECE
AHEAD = 5
CATCH = 2 * AHEAD
WIDE = 512


def wait_bytes(ref, sem):
    pltpu.make_async_copy(ref, ref, sem).wait()


def kernel(
    amps, ints, amp_gain, int_gain, occ, virt,
    out, whole_amps,
    own, whole_ints, high, low, chunk_in, split, stage,
    amp_send, amp_recv, int_send, int_recv, sib_send, sib_recv, out_send, out_recv, local, load,
):
    row, col = lax.axis_index("row"), lax.axis_index("col")
    y, core = row // 2, row % 2
    z, x = col // 4, col % 4

    def at(dy=0, dz=0, dx=0, dcore=0):
        r = lax.rem(y + dy, 4) * 2 + lax.rem(core + dcore, 2)
        return r, lax.rem(z + dz, 4) * 4 + lax.rem(x + dx, 4)

    sibling = at(dcore=1)
    y_next, y_prev = at(dy=1), at(dy=3)
    x_near = (at(dx=1), at(dx=3))
    z_near = (at(dz=1), at(dz=3))
    first, second = (x_near, z_near), (z_near, x_near)
    partners = [*x_near, *z_near, sibling] + [at(dy=d, dcore=c) for d in (1, 2, 3) for c in (0, 1)]

    barrier = pltpu.get_barrier_semaphore()
    for partner in partners:
        pl.semaphore_signal(barrier, inc=1, device_id=partner, device_id_type=MESH)
    pl.semaphore_wait(barrier, len(partners))

    def remote(src, dst, send, recv, device):
        pltpu.make_async_remote_copy(
            src_ref=src, dst_ref=dst, send_sem=send, recv_sem=recv, device_id=device, device_id_type=MESH
        ).start()

    def rows_of(c, part=None):
        if part is None:
            return pl.ds(pl.multiple_of(c * CHUNK, CHUNK), CHUNK)
        return pl.ds(pl.multiple_of(c * CHUNK + part * HALF, HALF), HALF)

    def block(way, dz, dx, rows):
        return whole_amps.at[way, lax.rem(z + dz, 4), lax.rem(x + dx, 4), rows, :]

    def bundle(way, d, rows):
        if way == 0:
            return whole_amps.at[0, lax.rem(z + d, 4), :, rows, :]
        return whole_amps.at[1, :, lax.rem(x + d, 4), rows, :]

    def near(way, d, rows):
        return block(way, 0, d, rows) if way == 0 else block(way, d, 0, rows)

    def step1(c):
        rows = rows_of(c)
        for way in (0, 1):
            for e in (0, 1):
                remote(own.at[way, rows, :], block(way, 0, 0, rows), amp_send.at[way, 0, e], amp_recv.at[way, 0, e, c], first[way][e])

    def step2(c):
        for way in (0, 1):
            for e in (0, 1):
                d = 3 if e == 0 else 1
                wait_bytes(near(way, d, rows_of(c)), amp_recv.at[way, 0, e, c])
                part = near(way, d, rows_of(c, e))
                remote(part, part, amp_send.at[way, 1, e], amp_recv.at[way, 1, e, c], first[way][e])

    def step3(c):
        for way in (0, 1):
            for e in (0, 1):
                wait_bytes(near(way, 2, rows_of(c, e)), amp_recv.at[way, 1, e, c])
            line = bundle(way, 0, rows_of(c))
            for e in (0, 1):
                remote(line, line, amp_send.at[way, 2, e], amp_recv.at[way, 2, e, c], second[way][e])

    def step4(c):
        for way in (0, 1):
            for e in (0, 1):
                d = 3 if e == 0 else 1
                wait_bytes(bundle(way, d, rows_of(c)), amp_recv.at[way, 2, e, c])
                part = bundle(way, d, rows_of(c, e))
                remote(part, part, amp_send.at[way, 3, e], amp_recv.at[way, 3, e, c], second[way][e])

    def step5(c):
        for way in (0, 1):
            for e in (0, 1):
                wait_bytes(bundle(way, 2, rows_of(c, e)), amp_recv.at[way, 3, e, c])

    def tick(t):
        for lead, step in ((4, step1), (3, step2), (2, step3), (1, step4), (0, step5)):
            c = t + lead
            pl.when((c >= (4 if lead == 4 else 0)) & (c < CHUNKS))(functools.partial(step, c))

    def int_rows(p, part=None):
        if part is None:
            return pl.ds(pl.multiple_of(p * PIECE, PIECE), PIECE)
        return pl.ds(pl.multiple_of(p * PIECE + part * (PIECE // 2), PIECE // 2), PIECE // 2)

    def int_block(dy, dcore, rows):
        return whole_ints.at[lax.rem(y + dy, 4) * 2 + lax.rem(core + dcore, 2), rows, :]

    def halve(dy, dcore, rows_at, count):
        b = lax.rem(y + dy, 4) * 2 + lax.rem(core + dcore, 2)
        value = whole_ints[b, pl.ds(rows_at, count), :]
        top = value.astype(BF16)
        rows = pl.ds(pl.multiple_of(b * 512 + rows_at, count), count)
        high[rows, :] = top
        low[rows, :] = (value - top.astype(F32)).astype(BF16)

    def int_start(p):
        rows = int_rows(p)
        piece = int_block(0, 0, rows)
        remote(piece, piece, int_send.at[0], int_recv.at[0, p], y_next)
        remote(piece, piece, int_send.at[1], int_recv.at[1, p], y_prev)
        remote(piece, piece, sib_send, sib_recv.at[0, p], sibling)

    def int_pass(p):
        rows = int_rows(p)
        for e, d, device in ((0, 3, y_next), (1, 1, y_prev)):
            piece = int_block(d, 0, rows)
            wait_bytes(piece, int_recv.at[e, p])
            part = int_block(d, 0, int_rows(p, e))
            remote(part, part, int_send.at[2 + e], int_recv.at[2 + e, p], device)
            remote(piece, piece, sib_send, sib_recv.at[1 + e, p], sibling)

    def int_near(p):
        base = pl.multiple_of(p * PIECE, PIECE)
        halve(0, 0, base, PIECE)
        halve(3, 0, base, PIECE)
        halve(1, 0, base, PIECE)

    def int_sibling(p):
        rows, base = int_rows(p), pl.multiple_of(p * PIECE, PIECE)
        for k, d in ((0, 0), (1, 3), (2, 1)):
            wait_bytes(int_block(d, 1, rows), sib_recv.at[k, p])
            halve(d, 1, base, PIECE)

    def int_far(p):
        rows, base = int_rows(p), pl.multiple_of(p * PIECE, PIECE)
        for e in (0, 1):
            wait_bytes(int_block(2, 0, int_rows(p, e)), int_recv.at[2 + e, p])
        piece = int_block(2, 0, rows)
        remote(piece, piece, sib_send, sib_recv.at[3, p], sibling)
        halve(2, 0, base, PIECE)

    def int_far_sibling(p):
        wait_bytes(int_block(2, 1, int_rows(p)), sib_recv.at[3, p])
        halve(2, 1, pl.multiple_of(p * PIECE, PIECE), PIECE)

    def mask_chunk(c):
        for k in range(CHUNK // TILE):
            rows = pl.ds(pl.multiple_of(c * CHUNK + k * TILE, TILE), TILE)
            gain = amp_gain[pl.ds(c * (CHUNK // TILE) + k, 1), :]
            value = amps[rows, :] * gain
            own[0, rows, :] = value[:, :128]
            own[1, rows, :] = value[:, 128:]

    for c in range(4):
        mask_chunk(c)
        step1(c)

    @pl.loop(0, PIECES)
    def _(p):
        rows = int_rows(p)
        whole_ints[row, rows, :] = ints[rows, :] * int_gain[pl.ds(p, 1), :]
        int_start(p)

    @pl.loop(4, CHUNKS)
    def _(c):
        mask_chunk(c)

    for way in (0, 1):
        pltpu.make_async_copy(own.at[way], whole_amps.at[way, z, x], local.at[way]).start()
    for way in (0, 1):
        pltpu.make_async_copy(own.at[way], whole_amps.at[way, z, x], local.at[way]).wait()

    @pl.loop(0, 3)
    def _(t):
        tick(t - 3)

    @pl.loop(0, AHEAD - 1)
    def _(t):
        tick(t)
        for q in (0, 1):
            int_pass(2 * t + q)
        for q in (0, 1):
            int_near(2 * t + q)

        @pl.when(t > 0)
        def _():
            for q in (0, 1):
                int_sibling(2 * t - 2 + q)

    tick(AHEAD - 1)
    for q in (0, 1):
        int_sibling(2 * (AHEAD - 2) + q)

    @pl.loop(0, PIECES // 2)
    def _(p):
        int_far(p)

    tick(AHEAD)

    @pl.loop(PIECES // 2, PIECES)
    def _(p):
        int_far(p)
        int_far_sibling(p - PIECES // 2)

    @pl.loop(PIECES // 2, PIECES)
    def _(p):
        int_far_sibling(p)

    def fetch(c):
        slot = lax.rem(c, 2)
        return pltpu.make_async_copy(whole_amps.at[:, :, :, rows_of(c), :], chunk_in.at[slot], load.at[slot])

    @pl.loop(0, CHUNKS)
    def _(c):
        @pl.when((c > 0) & ((c >= CATCH) | (lax.rem(c, 2) == 0)))
        def _():
            tick(jnp.where(c < CATCH, AHEAD + c // 2, c))

        @pl.when((c == 0) | (c >= CATCH))
        def _():
            fetch(c).start()

        fetch(c).wait()

        @pl.when(c < CATCH - 1)
        def _():
            fetch(c + 1).start()

        slot = lax.rem(c, 2)

        @pl.loop(0, 16)
        def _(k):
            value = jnp.concatenate([chunk_in[slot, 0, k // 4, lax.rem(k, 4)], chunk_in[slot, 1, k // 4, lax.rem(k, 4)]], axis=1)
            top = value.astype(BF16)
            at_k = pl.ds(pl.multiple_of(k * 256, 256), 256)
            split[pl.ds(0, CHUNK), at_k] = top
            split[pl.ds(CHUNK, CHUNK), at_k] = (value - top.astype(F32)).astype(BF16)

        rows = rows_of(c)

        @pl.loop(0, COLS // WIDE)
        def _(n):
            wide = pl.ds(pl.multiple_of(n * WIDE, WIDE), WIDE)
            both = jnp.dot(split[...], high[:, wide], preferred_element_type=F32)
            rest = jnp.dot(split[pl.ds(0, CHUNK)], low[:, wide], preferred_element_type=F32)
            scaled = (both[:CHUNK] + (both[CHUNK:] + rest)) / (occ[rows, :] + virt[:, wide])
            for q in range(WIDE // 128):
                stage[n * (WIDE // 128) + q, rows, :] = scaled[:, q * 128:(q + 1) * 128]

        there = pl.ds(pl.multiple_of(row * ROWS + c * CHUNK, CHUNK), CHUNK)
        for d in (4, 5, 2, 3, 6, 7, 1):
            owner = lax.rem(row + d, 8)
            remote(stage.at[owner, rows, :], out.at[there, :], out_send, out_recv.at[row], (owner, col))
        pltpu.make_async_copy(stage.at[row, rows, :], out.at[there, :], out_recv.at[row]).start()

    for source in range(8):
        wait_bytes(out.at[pl.ds(source * ROWS, ROWS), :], out_recv.at[source])
    wait_bytes(stage.at[pl.ds(0, 7)], out_send)
    for way in (0, 1):
        for e in (0, 1):
            wait_bytes(whole_amps.at[way, 0, 0], amp_send.at[way, 0, e])
            wait_bytes(whole_amps.at[way, 0, 0, pl.ds(0, ROWS // 2)], amp_send.at[way, 1, e])
            wait_bytes(whole_amps.at[way, 0], amp_send.at[way, 2, e])
            wait_bytes(whole_amps.at[way, 0, pl.ds(0, 2)], amp_send.at[way, 3, e])
    for e in (0, 1):
        wait_bytes(whole_ints.at[0], int_send.at[e])
        wait_bytes(whole_ints.at[0, pl.ds(0, 256)], int_send.at[2 + e])
    wait_bytes(whole_ints.at[pl.ds(0, 4)], sib_send)


def shards(amplitudes, integrals, amp_mask, int_mask, occ_shift, virt_shift):
    amp_gain = jnp.repeat(amp_mask.astype(F32), TILE, axis=1)
    int_gain = jnp.repeat(int_mask.astype(F32), TILE, axis=1)
    dma = pltpu.SemaphoreType.DMA
    vmem, anywhere = pl.BlockSpec(memory_space=pltpu.VMEM), pl.BlockSpec(memory_space=pl.ANY)
    out, _ = pl.pallas_call(
        kernel,
        name="ladder",
        out_shape=(
            jax.ShapeDtypeStruct((8 * ROWS, 128), F32),
            jax.ShapeDtypeStruct((2, 4, 4, ROWS, 128), F32),
        ),
        in_specs=[vmem] * 6,
        out_specs=(anywhere, anywhere),
        scratch_shapes=[
            pltpu.VMEM((2, ROWS, 128), F32),
            pltpu.VMEM((8, 512, COLS), F32),
            pltpu.VMEM((DEPTH, COLS), BF16),
            pltpu.VMEM((DEPTH, COLS), BF16),
            pltpu.VMEM((2, 2, 4, 4, CHUNK, 128), F32),
            pltpu.VMEM((2 * CHUNK, DEPTH), BF16),
            pltpu.VMEM((8, ROWS, 128), F32),
            dma((2, 4, 2)),
            dma((2, 4, 2, CHUNKS)),
            dma((4,)),
            dma((4, PIECES)),
            dma,
            dma((4, PIECES)),
            dma,
            dma((8,)),
            dma((2,)),
            dma((2,)),
        ],
        compiler_params=pltpu.CompilerParams(collective_id=0, has_side_effects=True, vmem_limit_bytes=60 << 20),
        cost_estimate=pl.CostEstimate(flops=6 * ROWS * DEPTH * COLS, bytes_accessed=80 << 20, transcendentals=0),
    )(amplitudes, integrals, amp_gain, int_gain, occ_shift[:, None], virt_shift[None, :])
    return out


def solution(mesh):
    placed = (
        P("row", "col"),
        P("row", "col"),
        P("row", "col"),
        P("row", "col"),
        P("row"),
        P("col"),
    )
    return jax.shard_map(
        shards, mesh=mesh, in_specs=placed, out_specs=P(None, ("col", "row")), check_vma=False
    )
```

```python
import functools

import jax
import jax.numpy as jnp
from jax import lax
from jax.experimental import pallas as pl
from jax.experimental.pallas import tpu as pltpu
from jax.sharding import PartitionSpec as P

MESH = pl.DeviceIdType.MESH
F32, BF16 = jnp.float32, jnp.bfloat16
TILE = 64
ROWS, DEPTH, COLS = 2048, 4096, 1024
CHUNK = 128
CHUNKS = ROWS // CHUNK
HALF = CHUNK // 2
PIECE = 64
PIECES = 512 // PIECE
AHEAD = 5
CATCH = 2 * AHEAD
WIDE = 512


def wait_bytes(ref, sem):
    pltpu.make_async_copy(ref, ref, sem).wait()


def whole_kernel(
    amps, ints, amp_gain, int_gain, occ, virt,
    out, whole_amps,
    own, whole_ints, high, low, chunk_in, split, stage,
    amp_send, amp_recv, int_send, int_recv, sib_send, sib_recv, out_send, out_recv, local, load,
):
    row, col = lax.axis_index("row"), lax.axis_index("col")
    y, core = row // 2, row % 2
    z, x = col // 4, col % 4

    def at(dy=0, dz=0, dx=0, dcore=0):
        r = lax.rem(y + dy, 4) * 2 + lax.rem(core + dcore, 2)
        return r, lax.rem(z + dz, 4) * 4 + lax.rem(x + dx, 4)

    sibling = at(dcore=1)
    y_next, y_prev = at(dy=1), at(dy=3)
    x_near = (at(dx=1), at(dx=3))
    z_near = (at(dz=1), at(dz=3))
    first, second = (x_near, z_near), (z_near, x_near)
    partners = [*x_near, *z_near, sibling] + [at(dy=d, dcore=c) for d in (1, 2, 3) for c in (0, 1)]

    barrier = pltpu.get_barrier_semaphore()
    for partner in partners:
        pl.semaphore_signal(barrier, inc=1, device_id=partner, device_id_type=MESH)
    pl.semaphore_wait(barrier, len(partners))

    def remote(src, dst, send, recv, device):
        pltpu.make_async_remote_copy(
            src_ref=src, dst_ref=dst, send_sem=send, recv_sem=recv, device_id=device, device_id_type=MESH
        ).start()

    def rows_of(c, part=None):
        if part is None:
            return pl.ds(pl.multiple_of(c * CHUNK, CHUNK), CHUNK)
        return pl.ds(pl.multiple_of(c * CHUNK + part * HALF, HALF), HALF)

    def block(way, dz, dx, rows):
        return whole_amps.at[way, lax.rem(z + dz, 4), lax.rem(x + dx, 4), rows, :]

    def bundle(way, d, rows):
        if way == 0:
            return whole_amps.at[0, lax.rem(z + d, 4), :, rows, :]
        return whole_amps.at[1, :, lax.rem(x + d, 4), rows, :]

    def near(way, d, rows):
        return block(way, 0, d, rows) if way == 0 else block(way, d, 0, rows)

    def step1(c):
        rows = rows_of(c)
        for way in (0, 1):
            for e in (0, 1):
                remote(own.at[way, rows, :], block(way, 0, 0, rows), amp_send.at[way, 0, e], amp_recv.at[way, 0, e, c], first[way][e])

    def step2(c):
        for way in (0, 1):
            for e in (0, 1):
                d = 3 if e == 0 else 1
                wait_bytes(near(way, d, rows_of(c)), amp_recv.at[way, 0, e, c])
                part = near(way, d, rows_of(c, e))
                remote(part, part, amp_send.at[way, 1, e], amp_recv.at[way, 1, e, c], first[way][e])

    def step3(c):
        for way in (0, 1):
            for e in (0, 1):
                wait_bytes(near(way, 2, rows_of(c, e)), amp_recv.at[way, 1, e, c])
            line = bundle(way, 0, rows_of(c))
            for e in (0, 1):
                remote(line, line, amp_send.at[way, 2, e], amp_recv.at[way, 2, e, c], second[way][e])

    def step4(c):
        for way in (0, 1):
            for e in (0, 1):
                d = 3 if e == 0 else 1
                wait_bytes(bundle(way, d, rows_of(c)), amp_recv.at[way, 2, e, c])
                part = bundle(way, d, rows_of(c, e))
                remote(part, part, amp_send.at[way, 3, e], amp_recv.at[way, 3, e, c], second[way][e])

    def step5(c):
        for way in (0, 1):
            for e in (0, 1):
                wait_bytes(bundle(way, 2, rows_of(c, e)), amp_recv.at[way, 3, e, c])

    def tick(t):
        for lead, step in ((4, step1), (3, step2), (2, step3), (1, step4), (0, step5)):
            c = t + lead
            pl.when((c >= (4 if lead == 4 else 0)) & (c < CHUNKS))(functools.partial(step, c))

    def int_rows(p, part=None):
        if part is None:
            return pl.ds(pl.multiple_of(p * PIECE, PIECE), PIECE)
        return pl.ds(pl.multiple_of(p * PIECE + part * (PIECE // 2), PIECE // 2), PIECE // 2)

    def int_block(dy, dcore, rows):
        return whole_ints.at[lax.rem(y + dy, 4) * 2 + lax.rem(core + dcore, 2), rows, :]

    def halve(dy, dcore, rows_at, count):
        b = lax.rem(y + dy, 4) * 2 + lax.rem(core + dcore, 2)
        value = whole_ints[b, pl.ds(rows_at, count), :]
        top = value.astype(BF16)
        rows = pl.ds(pl.multiple_of(b * 512 + rows_at, count), count)
        high[rows, :] = top
        low[rows, :] = (value - top.astype(F32)).astype(BF16)

    def int_start(p):
        rows = int_rows(p)
        piece = int_block(0, 0, rows)
        remote(piece, piece, int_send.at[0], int_recv.at[0, p], y_next)
        remote(piece, piece, int_send.at[1], int_recv.at[1, p], y_prev)
        remote(piece, piece, sib_send, sib_recv.at[0, p], sibling)

    def int_pass(p):
        rows = int_rows(p)
        for e, d, device in ((0, 3, y_next), (1, 1, y_prev)):
            piece = int_block(d, 0, rows)
            wait_bytes(piece, int_recv.at[e, p])
            part = int_block(d, 0, int_rows(p, e))
            remote(part, part, int_send.at[2 + e], int_recv.at[2 + e, p], device)
            remote(piece, piece, sib_send, sib_recv.at[1 + e, p], sibling)

    def int_near(p):
        base = pl.multiple_of(p * PIECE, PIECE)
        halve(0, 0, base, PIECE)
        halve(3, 0, base, PIECE)
        halve(1, 0, base, PIECE)

    def int_sibling(p):
        rows, base = int_rows(p), pl.multiple_of(p * PIECE, PIECE)
        for k, d in ((0, 0), (1, 3), (2, 1)):
            wait_bytes(int_block(d, 1, rows), sib_recv.at[k, p])
            halve(d, 1, base, PIECE)

    def int_far(p):
        rows, base = int_rows(p), pl.multiple_of(p * PIECE, PIECE)
        for e in (0, 1):
            wait_bytes(int_block(2, 0, int_rows(p, e)), int_recv.at[2 + e, p])
        piece = int_block(2, 0, rows)
        remote(piece, piece, sib_send, sib_recv.at[3, p], sibling)
        halve(2, 0, base, PIECE)

    def int_far_sibling(p):
        wait_bytes(int_block(2, 1, int_rows(p)), sib_recv.at[3, p])
        halve(2, 1, pl.multiple_of(p * PIECE, PIECE), PIECE)

    def mask_chunk(c):
        for k in range(CHUNK // TILE):
            rows = pl.ds(pl.multiple_of(c * CHUNK + k * TILE, TILE), TILE)
            gain = amp_gain[pl.ds(c * (CHUNK // TILE) + k, 1), :]
            value = amps[rows, :] * gain
            own[0, rows, :] = value[:, :128]
            own[1, rows, :] = value[:, 128:]

    for c in range(4):
        mask_chunk(c)
        step1(c)

    @pl.loop(0, PIECES)
    def _(p):
        rows = int_rows(p)
        whole_ints[row, rows, :] = ints[rows, :] * int_gain[pl.ds(p, 1), :]
        int_start(p)

    @pl.loop(4, CHUNKS)
    def _(c):
        mask_chunk(c)

    for way in (0, 1):
        pltpu.make_async_copy(own.at[way], whole_amps.at[way, z, x], local.at[way]).start()
    for way in (0, 1):
        pltpu.make_async_copy(own.at[way], whole_amps.at[way, z, x], local.at[way]).wait()

    @pl.loop(0, 3)
    def _(t):
        tick(t - 3)

    @pl.loop(0, AHEAD - 1)
    def _(t):
        tick(t)
        for q in (0, 1):
            int_pass(2 * t + q)
        for q in (0, 1):
            int_near(2 * t + q)

        @pl.when(t > 0)
        def _():
            for q in (0, 1):
                int_sibling(2 * t - 2 + q)

    tick(AHEAD - 1)
    for q in (0, 1):
        int_sibling(2 * (AHEAD - 2) + q)

    @pl.loop(0, PIECES // 2)
    def _(p):
        int_far(p)

    tick(AHEAD)

    @pl.loop(PIECES // 2, PIECES)
    def _(p):
        int_far(p)
        int_far_sibling(p - PIECES // 2)

    @pl.loop(PIECES // 2, PIECES)
    def _(p):
        int_far_sibling(p)

    def fetch(c):
        slot = lax.rem(c, 2)
        return pltpu.make_async_copy(whole_amps.at[:, :, :, rows_of(c), :], chunk_in.at[slot], load.at[slot])

    @pl.loop(0, CHUNKS)
    def _(c):
        @pl.when((c > 0) & ((c >= CATCH) | (lax.rem(c, 2) == 0)))
        def _():
            tick(jnp.where(c < CATCH, AHEAD + c // 2, c))

        @pl.when((c == 0) | (c >= CATCH))
        def _():
            fetch(c).start()

        fetch(c).wait()

        @pl.when(c < CATCH - 1)
        def _():
            fetch(c + 1).start()

        slot = lax.rem(c, 2)

        @pl.loop(0, 16)
        def _(k):
            value = jnp.concatenate([chunk_in[slot, 0, k // 4, lax.rem(k, 4)], chunk_in[slot, 1, k // 4, lax.rem(k, 4)]], axis=1)
            top = value.astype(BF16)
            at_k = pl.ds(pl.multiple_of(k * 256, 256), 256)
            split[pl.ds(0, CHUNK), at_k] = top
            split[pl.ds(CHUNK, CHUNK), at_k] = (value - top.astype(F32)).astype(BF16)

        rows = rows_of(c)

        @pl.loop(0, COLS // WIDE)
        def _(n):
            wide = pl.ds(pl.multiple_of(n * WIDE, WIDE), WIDE)
            both = jnp.dot(split[...], high[:, wide], preferred_element_type=F32)
            rest = jnp.dot(split[pl.ds(0, CHUNK)], low[:, wide], preferred_element_type=F32)
            scaled = (both[:CHUNK] + (both[CHUNK:] + rest)) / (occ[rows, :] + virt[:, wide])
            for q in range(WIDE // 128):
                stage[n * (WIDE // 128) + q, rows, :] = scaled[:, q * 128:(q + 1) * 128]

        there = pl.ds(pl.multiple_of(row * ROWS + c * CHUNK, CHUNK), CHUNK)
        for d in (4, 5, 2, 3, 6, 7, 1):
            owner = lax.rem(row + d, 8)
            remote(stage.at[owner, rows, :], out.at[there, :], out_send, out_recv.at[row], (owner, col))
        pltpu.make_async_copy(stage.at[row, rows, :], out.at[there, :], out_recv.at[row]).start()

    for source in range(8):
        wait_bytes(out.at[pl.ds(source * ROWS, ROWS), :], out_recv.at[source])
    wait_bytes(stage.at[pl.ds(0, 7)], out_send)
    for way in (0, 1):
        for e in (0, 1):
            wait_bytes(whole_amps.at[way, 0, 0], amp_send.at[way, 0, e])
            wait_bytes(whole_amps.at[way, 0, 0, pl.ds(0, ROWS // 2)], amp_send.at[way, 1, e])
            wait_bytes(whole_amps.at[way, 0], amp_send.at[way, 2, e])
            wait_bytes(whole_amps.at[way, 0, pl.ds(0, 2)], amp_send.at[way, 3, e])
    for e in (0, 1):
        wait_bytes(whole_ints.at[0], int_send.at[e])
        wait_bytes(whole_ints.at[0, pl.ds(0, 256)], int_send.at[2 + e])
    wait_bytes(whole_ints.at[pl.ds(0, 4)], sib_send)


def whole_ladder(amplitudes, integrals, amp_mask, int_mask, occ_shift, virt_shift):
    amp_gain = jnp.repeat(amp_mask.astype(F32), TILE, axis=1)
    int_gain = jnp.repeat(int_mask.astype(F32), TILE, axis=1)
    dma = pltpu.SemaphoreType.DMA
    vmem, anywhere = pl.BlockSpec(memory_space=pltpu.VMEM), pl.BlockSpec(memory_space=pl.ANY)
    out, _ = pl.pallas_call(
        whole_kernel,
        name="whole_ladder",
        out_shape=(
            jax.ShapeDtypeStruct((8 * ROWS, 128), F32),
            jax.ShapeDtypeStruct((2, 4, 4, ROWS, 128), F32),
        ),
        in_specs=[vmem] * 6,
        out_specs=(anywhere, anywhere),
        scratch_shapes=[
            pltpu.VMEM((2, ROWS, 128), F32),
            pltpu.VMEM((8, 512, COLS), F32),
            pltpu.VMEM((DEPTH, COLS), BF16),
            pltpu.VMEM((DEPTH, COLS), BF16),
            pltpu.VMEM((2, 2, 4, 4, CHUNK, 128), F32),
            pltpu.VMEM((2 * CHUNK, DEPTH), BF16),
            pltpu.VMEM((8, ROWS, 128), F32),
            dma((2, 4, 2)),
            dma((2, 4, 2, CHUNKS)),
            dma((4,)),
            dma((4, PIECES)),
            dma,
            dma((4, PIECES)),
            dma,
            dma((8,)),
            dma((2,)),
            dma((2,)),
        ],
        compiler_params=pltpu.CompilerParams(collective_id=1, has_side_effects=True, vmem_limit_bytes=60 << 20),
        cost_estimate=pl.CostEstimate(flops=6 * ROWS * DEPTH * COLS, bytes_accessed=80 << 20, transcendentals=0),
    )(amplitudes, integrals, amp_gain, int_gain, occ_shift[:, None], virt_shift[None, :])
    return out


MOST = 104
PAIRS = MOST // 4
STEPS = 13
STEP = PAIRS // STEPS
STEP_TILES = MOST // STEPS
NEED = (1, 2, 3, 4, 5, 6, 7, 7, 8, 9, 9, 10, 11, 12, 12, 13)
INT_MOST = 100
INT_PAIRS = INT_MOST // 2
INT_PIECES = 5
INT_PIECE = INT_PAIRS // INT_PIECES
SLOTS = 4
START = 5


def done_before(c):
    return jnp.minimum(STEPS, START + (10 * c) // 16)


def packed_kernel(
    amps, ints, tables, listing, occ, virt,
    out, over, whole_amps, whole_ints,
    own, own_ints, packed, int_a, int_b, high, low, split_a, split_b, stage, plane, ring, flags, plane_s, ring_s,
    amp_send, amp_recv, int_send, int_recv, sib_send, sib_recv, tab_send, tab_recv, out_send, out_self, out_recv, local, load,
    int_load, tab_load,
):
    row, col = lax.axis_index("row"), lax.axis_index("col")
    y, core = row // 2, row % 2
    z, x = col // 4, col % 4

    def at(dy=0, dz=0, dx=0, dcore=0):
        r = lax.rem(y + dy, 4) * 2 + lax.rem(core + dcore, 2)
        return r, lax.rem(z + dz, 4) * 4 + lax.rem(x + dx, 4)

    sibling = at(dcore=1)
    y_next, y_prev = at(dy=1), at(dy=3)
    x_near = (at(dx=1), at(dx=3))
    z_near = (at(dz=1), at(dz=3))
    first, second = (x_near, z_near), (z_near, x_near)
    partners = [*x_near, *z_near, sibling] + [at(dy=d, dcore=c) for d in (1, 2, 3) for c in (0, 1)]

    barrier = pltpu.get_barrier_semaphore()
    for partner in partners:
        pl.semaphore_signal(barrier, inc=1, device_id=partner, device_id_type=MESH)
    pl.semaphore_wait(barrier, len(partners))

    def remote(src, dst, send, recv, device):
        pltpu.make_async_remote_copy(
            src_ref=src, dst_ref=dst, send_sem=send, recv_sem=recv, device_id=device, device_id_type=MESH
        ).start()

    def plane_at(dz, dx):
        return plane.at[lax.rem(z + dz, 4), lax.rem(x + dx, 4)]

    def line_at(dz):
        return plane.at[lax.rem(z + dz, 4)]

    def ring_at(dy):
        return ring.at[lax.rem(y + dy, 4)]

    def tab(k, ref, device):
        remote(ref, ref, tab_send.at[k], tab_recv.at[k], device)

    def tab_wait(k, ref):
        wait_bytes(ref, tab_recv.at[k])

    def ring0():
        ring[y, core] = tables[...]
        tab(6, ring.at[y, core], sibling)

    def ring1():
        tab_wait(6, ring.at[y, 1 - core])
        tab(7, ring_at(0), y_next)
        tab(8, ring_at(0), y_prev)

    def ring2():
        tab_wait(7, ring_at(3))
        tab(9, ring_at(3), y_next)
        tab_wait(8, ring_at(1))

    def ring3():
        tab_wait(9, ring_at(2))
        pltpu.make_async_copy(ring, ring_s, tab_load).start()
        pltpu.make_async_copy(ring, ring_s, tab_load).wait()

    def plane0():
        plane[z, x] = tables[...]
        tab(0, plane_at(0, 0), x_near[0])
        tab(1, plane_at(0, 0), x_near[1])

    def plane1():
        tab_wait(0, plane_at(0, 3))
        tab(2, plane_at(0, 3), x_near[0])
        tab_wait(1, plane_at(0, 1))

    def plane2():
        tab_wait(2, plane_at(0, 2))
        tab(3, line_at(0), z_near[0])
        tab(4, line_at(0), z_near[1])

    def plane3():
        tab_wait(3, line_at(3))
        tab(5, line_at(3), z_near[0])
        tab_wait(4, line_at(1))

    def plane4():
        tab_wait(5, line_at(2))
        pltpu.make_async_copy(plane, plane_s, tab_load).start()
        pltpu.make_async_copy(plane, plane_s, tab_load).wait()

    def flag0():
        most = jnp.zeros((8, 128), jnp.int32)
        for zz in range(4):
            for xx in range(4):
                most = jnp.maximum(most, plane[zz, xx])
        flags[y, core] = most
        tab(10, flags.at[y, core], sibling)

    def flag1():
        tab_wait(10, flags.at[y, 1 - core])
        tab(11, flags.at[y], y_next)
        tab(12, flags.at[y], y_prev)

    def flag2():
        tab_wait(11, flags.at[lax.rem(y + 3, 4)])
        tab(13, flags.at[lax.rem(y + 3, 4)], y_next)
        tab_wait(12, flags.at[lax.rem(y + 1, 4)])

    def flag3():
        tab_wait(13, flags.at[lax.rem(y + 2, 4)])
        most = jnp.zeros((8, 128), jnp.int32)
        for yy in range(4):
            for cc in range(2):
                most = jnp.maximum(most, flags[yy, cc])
        over[...] = most

    def tab_end():
        for k, ref in enumerate((
            plane_at(0, 0), plane_at(0, 0), plane_at(0, 0), line_at(0), line_at(0), line_at(0), ring.at[0, 0], ring_at(0),
            ring_at(0), ring_at(0), flags.at[0, 0], flags.at[0], flags.at[0], flags.at[0],
        )):
            wait_bytes(ref, tab_send.at[k])

    lane = lax.broadcasted_iota(jnp.int32, (TILE, 128), 1)
    lane_row = lax.broadcasted_iota(jnp.int32, (1, 128), 1)

    def beside(left, right, left_kind, right_kind):
        kinds = jnp.where(lane_row < 64, left_kind, right_kind)
        straight = (kinds & 1).astype(F32)
        turned = (kinds >> 1).astype(F32)
        return (
            jnp.where(lane < 64, left, right) * straight
            + pltpu.roll(jnp.where(lane < 64, right, left), 64, 1) * turned
        )

    def rows_of(c, part=None):
        return pl.ds(c * STEP, STEP) if part is None else pl.ds(c * STEP + part, 1)

    def block(way, dz, dx, rows):
        return whole_amps.at[way, lax.rem(z + dz, 4), lax.rem(x + dx, 4), rows]

    def bundle(way, d, rows):
        if way == 0:
            return whole_amps.at[0, lax.rem(z + d, 4), :, rows]
        return whole_amps.at[1, :, lax.rem(x + d, 4), rows]

    def near(way, d, rows):
        return block(way, 0, d, rows) if way == 0 else block(way, d, 0, rows)

    def step1(c):
        rows = rows_of(c)
        for way in (0, 1):
            for e in (0, 1):
                remote(own.at[way, rows], block(way, 0, 0, rows), amp_send.at[way, 0, e], amp_recv.at[way, 0, e, c], first[way][e])

    def step2(c):
        for way in (0, 1):
            for e in (0, 1):
                d = 3 if e == 0 else 1
                wait_bytes(near(way, d, rows_of(c)), amp_recv.at[way, 0, e, c])
                part = near(way, d, rows_of(c, e))
                remote(part, part, amp_send.at[way, 1, e], amp_recv.at[way, 1, e, c], first[way][e])

    def step3(c):
        for way in (0, 1):
            for e in (0, 1):
                wait_bytes(near(way, 2, rows_of(c, e)), amp_recv.at[way, 1, e, c])
            line = bundle(way, 0, rows_of(c))
            for e in (0, 1):
                remote(line, line, amp_send.at[way, 2, e], amp_recv.at[way, 2, e, c], second[way][e])

    def step4(c):
        for way in (0, 1):
            for e in (0, 1):
                d = 3 if e == 0 else 1
                wait_bytes(bundle(way, d, rows_of(c)), amp_recv.at[way, 2, e, c])
                part = bundle(way, d, rows_of(c, e))
                remote(part, part, amp_send.at[way, 3, e], amp_recv.at[way, 3, e, c], second[way][e])

    def step5(c):
        for way in (0, 1):
            for e in (0, 1):
                wait_bytes(bundle(way, 2, rows_of(c, e)), amp_recv.at[way, 3, e, c])

    def tick(t):
        for lead, step in ((8, step1), (6, step2), (4, step3), (2, step4), (0, step5)):
            c = t + lead
            pl.when((c >= (8 if lead == 8 else 0)) & (c < STEPS))(functools.partial(step, c))

    def fetch(s):
        rows = rows_of(s)
        return pltpu.make_async_copy(whole_amps.at[:, :, :, rows], packed.at[:, :, :, rows], load)

    def int_rows(p, part=None):
        half = INT_PIECE // 2
        return pl.ds(p * INT_PIECE, INT_PIECE) if part is None else pl.ds(p * INT_PIECE + part * half, half)

    def int_block(dy, dcore, rows):
        return whole_ints.at[lax.rem(y + dy, 4) * 2 + lax.rem(core + dcore, 2), rows]

    def unpack_ints(ref, dy, dcore):
        yy, cc = lax.rem(y + dy, 4), lax.rem(core + dcore, 2)

        @pl.loop(0, 8)
        def _(t):
            rows = pl.ds(pl.multiple_of((yy * 2 + cc) * 512 + t * TILE, TILE), TILE)
            for g in range(8):
                one = t * 16 + 2 * g
                two = one + 1
                value = beside(
                    ref[ring_s[yy, cc, 3, one]], ref[ring_s[yy, cc, 3, two]], ring_s[yy, cc, 4, one], ring_s[yy, cc, 4, two]
                )
                top = value.astype(BF16)
                high[rows, g * 128:(g + 1) * 128] = top
                low[rows, g * 128:(g + 1) * 128] = (value - top.astype(F32)).astype(BF16)

    def int_start(p):
        rows = int_rows(p)
        piece, there = own_ints.at[rows], int_block(0, 0, rows)
        remote(piece, there, int_send.at[0], int_recv.at[0, p], y_next)
        remote(piece, there, int_send.at[1], int_recv.at[1, p], y_prev)

    def int_pass(p):
        rows = int_rows(p)
        for e, d, device in ((0, 3, y_next), (1, 1, y_prev)):
            piece = int_block(d, 0, rows)
            wait_bytes(piece, int_recv.at[e, p])
            part = int_block(d, 0, int_rows(p, e))
            remote(part, part, int_send.at[2 + e], int_recv.at[2 + e, p], device)
            remote(piece, piece, sib_send, sib_recv.at[1 + e, p], sibling)

    def int_in(k, buffer, dy, dcore):
        if dcore:
            if k == 0:
                wait_bytes(int_block(0, 1, pl.ds(0, INT_PAIRS)), sib_recv.at[0, 0])
            else:
                @pl.loop(0, INT_PIECES)
                def _(p):
                    wait_bytes(int_block(dy, 1, int_rows(p)), sib_recv.at[k, p])
        copy = pltpu.make_async_copy(int_block(dy, dcore, pl.ds(0, INT_PAIRS)), buffer, int_load.at[0 if buffer is int_a else 1])
        copy.start()
        return copy

    def int_far(p):
        for e in (0, 1):
            wait_bytes(int_block(2, 0, int_rows(p, e)), int_recv.at[2 + e, p])
        piece = int_block(2, 0, int_rows(p))
        remote(piece, piece, sib_send, sib_recv.at[3, p], sibling)

    ring0()
    plane0()

    @pl.loop(0, PAIRS)
    def _(i):
        for way in (0, 1):
            pair = 2 * i + way
            tiles = []
            for place in (2 * pair, 2 * pair + 1):
                both = amps[listing[0, place]]
                tiles.append(both[:, :128] * listing[1, place].astype(F32) + both[:, 128:] * listing[2, place].astype(F32))
            own[way, i] = beside(*tiles, listing[3, 2 * pair], listing[3, 2 * pair + 1])

    for c in range(8):
        step1(c)
    ring1()

    for t in range(8):
        for g in range(8):
            stage[t // 2, g, t % 2] = ints[t * TILE:(t + 1) * TILE, g * 128:(g + 1) * 128]

    @pl.loop(0, INT_PAIRS)
    def _(pair):
        one = 2 * pair
        two = one + 1
        own_ints[pair] = beside(
            stage[listing[4, one], listing[5, one], listing[6, one]], stage[listing[4, two], listing[5, two], listing[6, two]],
            listing[7, one], listing[7, two],
        )

    ring2()

    @pl.loop(0, INT_PIECES)
    def _(p):
        int_start(p)

    remote(own_ints, int_block(0, 0, pl.ds(0, INT_PAIRS)), sib_send, sib_recv.at[0, 0], sibling)
    for way in (0, 1):
        pltpu.make_async_copy(own.at[way], whole_amps.at[way, z, x], local.at[way]).start()
    for way in (0, 1):
        pltpu.make_async_copy(own.at[way], whole_amps.at[way, z, x], local.at[way]).wait()

    tick(-6)
    plane1()
    tick(-5)
    tick(-4)
    plane2()
    tick(-3)
    ring3()
    tick(-2)
    unpack_ints(own_ints, 0, 0)
    plane3()
    tick(-1)
    other = int_in(0, int_a, 0, 1)
    tick(0)
    plane4()
    int_pass(0)
    flag0()
    other.wait()
    unpack_ints(int_a, 0, 1)
    int_pass(1)
    tick(1)
    flag1()
    int_pass(2)
    tick(2)
    int_pass(3)
    tick(3)
    int_pass(4)
    left, right = int_in(None, int_a, 3, 0), int_in(None, int_b, 1, 0)
    left.wait()
    unpack_ints(int_a, 3, 0)
    left = int_in(1, int_a, 3, 1)
    right.wait()
    unpack_ints(int_b, 1, 0)
    right = int_in(2, int_b, 1, 1)
    flag2()
    left.wait()
    unpack_ints(int_a, 3, 1)
    right.wait()
    unpack_ints(int_b, 1, 1)
    tick(4)

    @pl.loop(0, START)
    def _(s):
        fetch(s).start()

    @pl.loop(0, INT_PIECES)
    def _(p):
        int_far(p)

    left = int_in(None, int_a, 2, 0)
    wait_bytes(whole_amps.at[:, :, :, pl.ds(0, START * STEP)], load)
    left.wait()
    unpack_ints(int_a, 2, 0)
    right = int_in(3, int_b, 2, 1)
    right.wait()
    unpack_ints(int_b, 2, 1)

    def stage_wait(slot):
        wait_bytes(stage.at[slot, pl.ds(0, 7)], out_send.at[slot])
        wait_bytes(stage.at[slot, 0], out_self.at[slot])

    def unpack_amps(split, c, zz, xx, at_k):
        for t in (0, 1):
            for g in (0, 1):
                one = (c * 2 + t) * 4 + 2 * g
                two = one + 1
                value = beside(
                    packed[plane_s[zz, xx, 0, one], zz, xx, plane_s[zz, xx, 1, one]],
                    packed[plane_s[zz, xx, 0, two], zz, xx, plane_s[zz, xx, 1, two]],
                    plane_s[zz, xx, 2, one], plane_s[zz, xx, 2, two],
                )
                top = value.astype(BF16)
                lanes = pl.ds(pl.multiple_of(at_k + g * 128, 128), 128)
                split[t * TILE:(t + 1) * TILE, lanes] = top
                split[CHUNK + t * TILE:CHUNK + (t + 1) * TILE, lanes] = (value - top.astype(F32)).astype(BF16)

    @pl.loop(0, 16)
    def _(k):
        unpack_amps(split_a, 0, k // 4, lax.rem(k, 4), k * 256)

    def multiply(c, split, split_next):
        before, after = done_before(c), done_before(c + 1)

        @pl.when(after > before)
        def _():
            tick(after - 1)

        slot = lax.rem(c, SLOTS)
        pl.when(c >= SLOTS)(functools.partial(stage_wait, slot))
        shift = jnp.transpose(jnp.broadcast_to(occ[pl.ds(c, 1), :], (CHUNK, 128)))
        later = jnp.minimum(c + 1, CHUNKS - 1)

        @pl.loop(0, COLS // WIDE)
        def _(n):
            wide = pl.ds(pl.multiple_of(n * WIDE, WIDE), WIDE)
            both = jnp.dot(split[...], high[:, wide], preferred_element_type=F32)
            for k in range(8):
                unpack_amps(split_next, later, n * 2 + k // 4, k % 4, n * 2048 + k * 256)
            rest = jnp.dot(split[0:CHUNK], low[:, wide], preferred_element_type=F32)
            ladder = both[:CHUNK] + (both[CHUNK:] + rest)
            for q in range(WIDE // 128):
                at_q = n * (WIDE // 128) + q
                scaled = ladder[:, q * 128:(q + 1) * 128] / (shift + virt[pl.ds(at_q, 1), :])
                stage[slot, at_q, 0] = scaled[:TILE]
                stage[slot, at_q, 1] = scaled[TILE:]

        there = pl.ds(row * (ROWS // TILE) + c * (CHUNK // TILE), CHUNK // TILE)
        for d in (4, 5, 2, 3, 6, 7, 1):
            owner = lax.rem(row + d, 8)
            remote(stage.at[slot, owner], out.at[there], out_send.at[slot], out_recv.at[row], (owner, col))
        pltpu.make_async_copy(stage.at[slot, row], out.at[there], out_self.at[slot]).start()

        @pl.when(after > before)
        def _():
            fetch(after - 1).start()
            fetch(after - 1).wait()

    @pl.loop(0, CHUNKS // 2)
    def _(i):
        multiply(2 * i, split_a, split_b)
        multiply(2 * i + 1, split_b, split_a)

    flag3()
    for slot in range(SLOTS):
        stage_wait(slot)
    for d in range(1, 8):
        source = lax.rem(row + d, 8)
        wait_bytes(out.at[pl.ds(source * (ROWS // TILE), ROWS // TILE)], out_recv.at[source])
    for way in (0, 1):
        for e in (0, 1):
            wait_bytes(whole_amps.at[way, 0, 0], amp_send.at[way, 0, e])
            wait_bytes(whole_amps.at[way, 0, 0, pl.ds(0, PAIRS // 2)], amp_send.at[way, 1, e])
            wait_bytes(whole_amps.at[way, 0], amp_send.at[way, 2, e])
            wait_bytes(whole_amps.at[way, 0, pl.ds(0, 2)], amp_send.at[way, 3, e])
    for e in (0, 1):
        wait_bytes(whole_ints.at[0], int_send.at[e])
        wait_bytes(whole_ints.at[0, pl.ds(0, INT_PAIRS // 2)], int_send.at[2 + e])
    wait_bytes(whole_ints.at[pl.ds(0, 4)], sib_send)
    tab_end()


def packed_ladder(amplitudes, integrals, tables, listing, occ_shift, virt_shift):
    dma = pltpu.SemaphoreType.DMA
    vmem, anywhere = pl.BlockSpec(memory_space=pltpu.VMEM), pl.BlockSpec(memory_space=pl.ANY)
    out, over, _, _ = pl.pallas_call(
        packed_kernel,
        name="packed_ladder",
        out_shape=(
            jax.ShapeDtypeStruct((8 * ROWS // TILE, TILE, 128), F32),
            jax.ShapeDtypeStruct((8, 128), jnp.int32),
            jax.ShapeDtypeStruct((2, 4, 4, PAIRS, TILE, 128), F32),
            jax.ShapeDtypeStruct((8, INT_PAIRS, TILE, 128), F32),
        ),
        in_specs=[vmem] * 3 + [pl.BlockSpec(memory_space=pltpu.SMEM)] + [vmem] * 2,
        out_specs=(anywhere, vmem, anywhere, anywhere),
        scratch_shapes=[
            pltpu.VMEM((2, PAIRS, TILE, 128), F32),
            pltpu.VMEM((INT_PAIRS, TILE, 128), F32),
            pltpu.VMEM((2, 4, 4, PAIRS, TILE, 128), F32),
            pltpu.VMEM((INT_PAIRS, TILE, 128), F32),
            pltpu.VMEM((INT_PAIRS, TILE, 128), F32),
            pltpu.VMEM((DEPTH, COLS), BF16),
            pltpu.VMEM((DEPTH, COLS), BF16),
            pltpu.VMEM((2 * CHUNK, DEPTH), BF16),
            pltpu.VMEM((2 * CHUNK, DEPTH), BF16),
            pltpu.VMEM((SLOTS, 8, CHUNK // TILE, TILE, 128), F32),
            pltpu.VMEM((4, 4, 8, 128), jnp.int32),
            pltpu.VMEM((4, 2, 8, 128), jnp.int32),
            pltpu.VMEM((4, 2, 8, 128), jnp.int32),
            pltpu.SMEM((4, 4, 8, 128), jnp.int32),
            pltpu.SMEM((4, 2, 8, 128), jnp.int32),
            dma((2, 4, 2)),
            dma((2, 4, 2, STEPS)),
            dma((4,)),
            dma((4, INT_PIECES)),
            dma,
            dma((4, INT_PIECES)),
            dma((14,)),
            dma((14,)),
            dma((SLOTS,)),
            dma((SLOTS,)),
            dma((8,)),
            dma((2,)),
            dma,
            dma((2,)),
            dma,
        ],
        compiler_params=pltpu.CompilerParams(collective_id=0, has_side_effects=True, vmem_limit_bytes=61 << 20),
        cost_estimate=pl.CostEstimate(flops=6 * ROWS * DEPTH * COLS, bytes_accessed=80 << 20, transcendentals=0),
    )(
        amplitudes.reshape(ROWS // TILE, TILE, 256), integrals, tables, listing, occ_shift.reshape(CHUNKS, 128),
        virt_shift.reshape(8, 128),
    )
    return out.reshape(8 * ROWS, 128), over[5, 0]


def shards(amplitudes, integrals, amp_mask, int_mask, occ_shift, virt_shift):
    masks = jnp.stack([amp_mask.reshape(128), int_mask.reshape(128)])
    count = jnp.arange(128, dtype=jnp.int32)
    slots = jnp.sum(jnp.where(count[:, None] < count[None, :], masks[:, :, None], 0), axis=1)
    used = slots + masks
    room = jnp.array([STEP_TILES * n for n in NEED], jnp.int32)
    over = jnp.any(used[0].reshape(CHUNKS, 8)[:, 7] > room) | (used[1, 127] > INT_MOST)
    limit = jnp.array([[MOST - 1], [INT_MOST - 1]], jnp.int32)
    at = jnp.where(masks != 0, jnp.minimum(slots, limit), 0)
    kind = jnp.where(masks != 0, 1 + ((at ^ count[None, :]) & 1), 0)
    here = (masks[:, :, None] != 0) & (slots[:, :, None] == count[None, None, :])
    place = jnp.sum(jnp.where(here, count[None, :, None], 0), axis=1)
    turn = 1 + ((place ^ count[None, :]) & 1)
    flags = jnp.broadcast_to(over.astype(jnp.int32), (128,))
    tables = jnp.stack([(at[0] >> 1) & 1, at[0] >> 2, kind[0], at[1] >> 1, kind[1], flags, flags, flags])
    a, b = place
    listing = jnp.stack([
        a >> 2, 1 - ((a >> 1) & 1), (a >> 1) & 1, turn[0], b >> 5, (b >> 1) & 7, (b >> 4) & 1, turn[1]
    ])
    update, over = packed_ladder(amplitudes, integrals, tables, listing, occ_shift, virt_shift)
    return lax.cond(
        over > 0,
        lambda: whole_ladder(amplitudes, integrals, amp_mask, int_mask, occ_shift, virt_shift),
        lambda: update,
    )


def solution(mesh):
    placed = (
        P("row", "col"),
        P("row", "col"),
        P("row", "col"),
        P("row", "col"),
        P("row"),
        P("col"),
    )
    return jax.shard_map(
        shards, mesh=mesh, in_specs=placed, out_specs=P(None, ("col", "row")), check_vma=False
    )
```

```python
import functools

import jax
import jax.numpy as jnp
from jax import lax
from jax.experimental import pallas as pl
from jax.experimental.pallas import tpu as pltpu
from jax.sharding import PartitionSpec as P

MESH = pl.DeviceIdType.MESH
F32, BF16 = jnp.float32, jnp.bfloat16
TILE = 64
ROWS, DEPTH, COLS = 2048, 4096, 1024
CHUNK = 128
CHUNKS = ROWS // CHUNK
HALF = CHUNK // 2
PIECE = 64
PIECES = 512 // PIECE
AHEAD = 5
CATCH = 2 * AHEAD
WIDE = 512


def wait_bytes(ref, sem):
    pltpu.make_async_copy(ref, ref, sem).wait()


def whole_kernel(
    amps, ints, amp_gain, int_gain, occ, virt,
    out, whole_amps,
    own, whole_ints, high, low, chunk_in, split, stage,
    amp_send, amp_recv, int_send, int_recv, sib_send, sib_recv, out_send, out_recv, local, load,
):
    row, col = lax.axis_index("row"), lax.axis_index("col")
    y, core = row // 2, row % 2
    z, x = col // 4, col % 4

    def at(dy=0, dz=0, dx=0, dcore=0):
        r = lax.rem(y + dy, 4) * 2 + lax.rem(core + dcore, 2)
        return r, lax.rem(z + dz, 4) * 4 + lax.rem(x + dx, 4)

    sibling = at(dcore=1)
    y_next, y_prev = at(dy=1), at(dy=3)
    x_near = (at(dx=1), at(dx=3))
    z_near = (at(dz=1), at(dz=3))
    first, second = (x_near, z_near), (z_near, x_near)
    partners = [*x_near, *z_near, sibling] + [at(dy=d, dcore=c) for d in (1, 2, 3) for c in (0, 1)]

    barrier = pltpu.get_barrier_semaphore()
    for partner in partners:
        pl.semaphore_signal(barrier, inc=1, device_id=partner, device_id_type=MESH)
    pl.semaphore_wait(barrier, len(partners))

    def remote(src, dst, send, recv, device):
        pltpu.make_async_remote_copy(
            src_ref=src, dst_ref=dst, send_sem=send, recv_sem=recv, device_id=device, device_id_type=MESH
        ).start()

    def rows_of(c, part=None):
        if part is None:
            return pl.ds(pl.multiple_of(c * CHUNK, CHUNK), CHUNK)
        return pl.ds(pl.multiple_of(c * CHUNK + part * HALF, HALF), HALF)

    def block(way, dz, dx, rows):
        return whole_amps.at[way, lax.rem(z + dz, 4), lax.rem(x + dx, 4), rows, :]

    def bundle(way, d, rows):
        if way == 0:
            return whole_amps.at[0, lax.rem(z + d, 4), :, rows, :]
        return whole_amps.at[1, :, lax.rem(x + d, 4), rows, :]

    def near(way, d, rows):
        return block(way, 0, d, rows) if way == 0 else block(way, d, 0, rows)

    def step1(c):
        rows = rows_of(c)
        for way in (0, 1):
            for e in (0, 1):
                remote(own.at[way, rows, :], block(way, 0, 0, rows), amp_send.at[way, 0, e], amp_recv.at[way, 0, e, c], first[way][e])

    def step2(c):
        for way in (0, 1):
            for e in (0, 1):
                d = 3 if e == 0 else 1
                wait_bytes(near(way, d, rows_of(c)), amp_recv.at[way, 0, e, c])
                part = near(way, d, rows_of(c, e))
                remote(part, part, amp_send.at[way, 1, e], amp_recv.at[way, 1, e, c], first[way][e])

    def step3(c):
        for way in (0, 1):
            for e in (0, 1):
                wait_bytes(near(way, 2, rows_of(c, e)), amp_recv.at[way, 1, e, c])
            line = bundle(way, 0, rows_of(c))
            for e in (0, 1):
                remote(line, line, amp_send.at[way, 2, e], amp_recv.at[way, 2, e, c], second[way][e])

    def step4(c):
        for way in (0, 1):
            for e in (0, 1):
                d = 3 if e == 0 else 1
                wait_bytes(bundle(way, d, rows_of(c)), amp_recv.at[way, 2, e, c])
                part = bundle(way, d, rows_of(c, e))
                remote(part, part, amp_send.at[way, 3, e], amp_recv.at[way, 3, e, c], second[way][e])

    def step5(c):
        for way in (0, 1):
            for e in (0, 1):
                wait_bytes(bundle(way, 2, rows_of(c, e)), amp_recv.at[way, 3, e, c])

    def tick(t):
        for lead, step in ((4, step1), (3, step2), (2, step3), (1, step4), (0, step5)):
            c = t + lead
            pl.when((c >= (4 if lead == 4 else 0)) & (c < CHUNKS))(functools.partial(step, c))

    def int_rows(p, part=None):
        if part is None:
            return pl.ds(pl.multiple_of(p * PIECE, PIECE), PIECE)
        return pl.ds(pl.multiple_of(p * PIECE + part * (PIECE // 2), PIECE // 2), PIECE // 2)

    def int_block(dy, dcore, rows):
        return whole_ints.at[lax.rem(y + dy, 4) * 2 + lax.rem(core + dcore, 2), rows, :]

    def halve(dy, dcore, rows_at, count):
        b = lax.rem(y + dy, 4) * 2 + lax.rem(core + dcore, 2)
        value = whole_ints[b, pl.ds(rows_at, count), :]
        top = value.astype(BF16)
        rows = pl.ds(pl.multiple_of(b * 512 + rows_at, count), count)
        high[rows, :] = top
        low[rows, :] = (value - top.astype(F32)).astype(BF16)

    def int_start(p):
        rows = int_rows(p)
        piece = int_block(0, 0, rows)
        remote(piece, piece, int_send.at[0], int_recv.at[0, p], y_next)
        remote(piece, piece, int_send.at[1], int_recv.at[1, p], y_prev)
        remote(piece, piece, sib_send, sib_recv.at[0, p], sibling)

    def int_pass(p):
        rows = int_rows(p)
        for e, d, device in ((0, 3, y_next), (1, 1, y_prev)):
            piece = int_block(d, 0, rows)
            wait_bytes(piece, int_recv.at[e, p])
            part = int_block(d, 0, int_rows(p, e))
            remote(part, part, int_send.at[2 + e], int_recv.at[2 + e, p], device)
            remote(piece, piece, sib_send, sib_recv.at[1 + e, p], sibling)

    def int_near(p):
        base = pl.multiple_of(p * PIECE, PIECE)
        halve(0, 0, base, PIECE)
        halve(3, 0, base, PIECE)
        halve(1, 0, base, PIECE)

    def int_sibling(p):
        rows, base = int_rows(p), pl.multiple_of(p * PIECE, PIECE)
        for k, d in ((0, 0), (1, 3), (2, 1)):
            wait_bytes(int_block(d, 1, rows), sib_recv.at[k, p])
            halve(d, 1, base, PIECE)

    def int_far(p):
        rows, base = int_rows(p), pl.multiple_of(p * PIECE, PIECE)
        for e in (0, 1):
            wait_bytes(int_block(2, 0, int_rows(p, e)), int_recv.at[2 + e, p])
        piece = int_block(2, 0, rows)
        remote(piece, piece, sib_send, sib_recv.at[3, p], sibling)
        halve(2, 0, base, PIECE)

    def int_far_sibling(p):
        wait_bytes(int_block(2, 1, int_rows(p)), sib_recv.at[3, p])
        halve(2, 1, pl.multiple_of(p * PIECE, PIECE), PIECE)

    def mask_chunk(c):
        for k in range(CHUNK // TILE):
            rows = pl.ds(pl.multiple_of(c * CHUNK + k * TILE, TILE), TILE)
            gain = amp_gain[pl.ds(c * (CHUNK // TILE) + k, 1), :]
            value = amps[rows, :] * gain
            own[0, rows, :] = value[:, :128]
            own[1, rows, :] = value[:, 128:]

    for c in range(4):
        mask_chunk(c)
        step1(c)

    @pl.loop(0, PIECES)
    def _(p):
        rows = int_rows(p)
        whole_ints[row, rows, :] = ints[rows, :] * int_gain[pl.ds(p, 1), :]
        int_start(p)

    @pl.loop(4, CHUNKS)
    def _(c):
        mask_chunk(c)

    for way in (0, 1):
        pltpu.make_async_copy(own.at[way], whole_amps.at[way, z, x], local.at[way]).start()
    for way in (0, 1):
        pltpu.make_async_copy(own.at[way], whole_amps.at[way, z, x], local.at[way]).wait()

    @pl.loop(0, 3)
    def _(t):
        tick(t - 3)

    @pl.loop(0, AHEAD - 1)
    def _(t):
        tick(t)
        for q in (0, 1):
            int_pass(2 * t + q)
        for q in (0, 1):
            int_near(2 * t + q)

        @pl.when(t > 0)
        def _():
            for q in (0, 1):
                int_sibling(2 * t - 2 + q)

    tick(AHEAD - 1)
    for q in (0, 1):
        int_sibling(2 * (AHEAD - 2) + q)

    @pl.loop(0, PIECES // 2)
    def _(p):
        int_far(p)

    tick(AHEAD)

    @pl.loop(PIECES // 2, PIECES)
    def _(p):
        int_far(p)
        int_far_sibling(p - PIECES // 2)

    @pl.loop(PIECES // 2, PIECES)
    def _(p):
        int_far_sibling(p)

    def fetch(c):
        slot = lax.rem(c, 2)
        return pltpu.make_async_copy(whole_amps.at[:, :, :, rows_of(c), :], chunk_in.at[slot], load.at[slot])

    @pl.loop(0, CHUNKS)
    def _(c):
        @pl.when((c > 0) & ((c >= CATCH) | (lax.rem(c, 2) == 0)))
        def _():
            tick(jnp.where(c < CATCH, AHEAD + c // 2, c))

        @pl.when((c == 0) | (c >= CATCH))
        def _():
            fetch(c).start()

        fetch(c).wait()

        @pl.when(c < CATCH - 1)
        def _():
            fetch(c + 1).start()

        slot = lax.rem(c, 2)

        @pl.loop(0, 16)
        def _(k):
            value = jnp.concatenate([chunk_in[slot, 0, k // 4, lax.rem(k, 4)], chunk_in[slot, 1, k // 4, lax.rem(k, 4)]], axis=1)
            top = value.astype(BF16)
            at_k = pl.ds(pl.multiple_of(k * 256, 256), 256)
            split[pl.ds(0, CHUNK), at_k] = top
            split[pl.ds(CHUNK, CHUNK), at_k] = (value - top.astype(F32)).astype(BF16)

        rows = rows_of(c)

        @pl.loop(0, COLS // WIDE)
        def _(n):
            wide = pl.ds(pl.multiple_of(n * WIDE, WIDE), WIDE)
            both = jnp.dot(split[...], high[:, wide], preferred_element_type=F32)
            rest = jnp.dot(split[pl.ds(0, CHUNK)], low[:, wide], preferred_element_type=F32)
            scaled = (both[:CHUNK] + (both[CHUNK:] + rest)) / (occ[rows, :] + virt[:, wide])
            for q in range(WIDE // 128):
                stage[n * (WIDE // 128) + q, rows, :] = scaled[:, q * 128:(q + 1) * 128]

        there = pl.ds(pl.multiple_of(row * ROWS + c * CHUNK, CHUNK), CHUNK)
        for d in (4, 5, 2, 3, 6, 7, 1):
            owner = lax.rem(row + d, 8)
            remote(stage.at[owner, rows, :], out.at[there, :], out_send, out_recv.at[row], (owner, col))
        pltpu.make_async_copy(stage.at[row, rows, :], out.at[there, :], out_recv.at[row]).start()

    for source in range(8):
        wait_bytes(out.at[pl.ds(source * ROWS, ROWS), :], out_recv.at[source])
    wait_bytes(stage.at[pl.ds(0, 7)], out_send)
    for way in (0, 1):
        for e in (0, 1):
            wait_bytes(whole_amps.at[way, 0, 0], amp_send.at[way, 0, e])
            wait_bytes(whole_amps.at[way, 0, 0, pl.ds(0, ROWS // 2)], amp_send.at[way, 1, e])
            wait_bytes(whole_amps.at[way, 0], amp_send.at[way, 2, e])
            wait_bytes(whole_amps.at[way, 0, pl.ds(0, 2)], amp_send.at[way, 3, e])
    for e in (0, 1):
        wait_bytes(whole_ints.at[0], int_send.at[e])
        wait_bytes(whole_ints.at[0, pl.ds(0, 256)], int_send.at[2 + e])
    wait_bytes(whole_ints.at[pl.ds(0, 4)], sib_send)


def whole_ladder(amplitudes, integrals, amp_mask, int_mask, occ_shift, virt_shift):
    amp_gain = jnp.repeat(amp_mask.astype(F32), TILE, axis=1)
    int_gain = jnp.repeat(int_mask.astype(F32), TILE, axis=1)
    dma = pltpu.SemaphoreType.DMA
    vmem, anywhere = pl.BlockSpec(memory_space=pltpu.VMEM), pl.BlockSpec(memory_space=pl.ANY)
    out, _ = pl.pallas_call(
        whole_kernel,
        name="whole_ladder",
        out_shape=(
            jax.ShapeDtypeStruct((8 * ROWS, 128), F32),
            jax.ShapeDtypeStruct((2, 4, 4, ROWS, 128), F32),
        ),
        in_specs=[vmem] * 6,
        out_specs=(anywhere, anywhere),
        scratch_shapes=[
            pltpu.VMEM((2, ROWS, 128), F32),
            pltpu.VMEM((8, 512, COLS), F32),
            pltpu.VMEM((DEPTH, COLS), BF16),
            pltpu.VMEM((DEPTH, COLS), BF16),
            pltpu.VMEM((2, 2, 4, 4, CHUNK, 128), F32),
            pltpu.VMEM((2 * CHUNK, DEPTH), BF16),
            pltpu.VMEM((8, ROWS, 128), F32),
            dma((2, 4, 2)),
            dma((2, 4, 2, CHUNKS)),
            dma((4,)),
            dma((4, PIECES)),
            dma,
            dma((4, PIECES)),
            dma,
            dma((8,)),
            dma((2,)),
            dma((2,)),
        ],
        compiler_params=pltpu.CompilerParams(collective_id=1, has_side_effects=True, vmem_limit_bytes=60 << 20),
        cost_estimate=pl.CostEstimate(flops=6 * ROWS * DEPTH * COLS, bytes_accessed=80 << 20, transcendentals=0),
    )(amplitudes, integrals, amp_gain, int_gain, occ_shift[:, None], virt_shift[None, :])
    return out


MOST = 104
PAIRS = MOST // 4
STEPS = 13
STEP = PAIRS // STEPS
STEP_TILES = MOST // STEPS
NEED = (1, 2, 3, 4, 5, 6, 7, 7, 8, 9, 9, 10, 11, 12, 12, 13)
INT_MOST = 104
INT_PAIRS = INT_MOST // 2
INT_PIECES = 13
INT_PIECE = INT_PAIRS // INT_PIECES
INT_EARLY = 7
SLOTS = 8
EARLY = 6


def packed_kernel(
    amps, ints, tables, listing, occ, virt,
    out, over, whole_amps, whole_ints,
    own, own_ints, packed, int_a, int_b, high, low, split_a, split_b, stage, plane, ring, flags, plane_s, ring_s,
    amp_send, amp_recv, int_send, int_recv, sib_send, sib_recv, tab_send, tab_recv, out_send, out_self, out_recv, local, load,
    int_load, tab_load,
):
    row, col = lax.axis_index("row"), lax.axis_index("col")
    y, core = row // 2, row % 2
    z, x = col // 4, col % 4

    def at(dy=0, dz=0, dx=0, dcore=0):
        r = lax.rem(y + dy, 4) * 2 + lax.rem(core + dcore, 2)
        return r, lax.rem(z + dz, 4) * 4 + lax.rem(x + dx, 4)

    sibling = at(dcore=1)
    y_next, y_prev = at(dy=1), at(dy=3)
    x_near = (at(dx=1), at(dx=3))
    z_near = (at(dz=1), at(dz=3))
    first, second = (x_near, z_near), (z_near, x_near)
    partners = [*x_near, *z_near, sibling] + [at(dy=d, dcore=c) for d in (1, 2, 3) for c in (0, 1)]

    barrier = pltpu.get_barrier_semaphore()
    for partner in partners:
        pl.semaphore_signal(barrier, inc=1, device_id=partner, device_id_type=MESH)
    pl.semaphore_wait(barrier, len(partners))

    def remote(src, dst, send, recv, device):
        pltpu.make_async_remote_copy(
            src_ref=src, dst_ref=dst, send_sem=send, recv_sem=recv, device_id=device, device_id_type=MESH
        ).start()

    def plane_at(dz, dx):
        return plane.at[lax.rem(z + dz, 4), lax.rem(x + dx, 4)]

    def line_at(dz):
        return plane.at[lax.rem(z + dz, 4)]

    def ring_at(dy):
        return ring.at[lax.rem(y + dy, 4)]

    def tab(k, ref, device):
        remote(ref, ref, tab_send.at[k], tab_recv.at[k], device)

    def tab_wait(k, ref):
        wait_bytes(ref, tab_recv.at[k])

    def ring0():
        ring[y, core] = tables[...]
        tab(6, ring.at[y, core], sibling)

    def ring1():
        tab_wait(6, ring.at[y, 1 - core])
        tab(7, ring_at(0), y_next)
        tab(8, ring_at(0), y_prev)

    def ring2():
        tab_wait(7, ring_at(3))
        tab(9, ring_at(3), y_next)
        tab_wait(8, ring_at(1))

    def ring3():
        tab_wait(9, ring_at(2))
        pltpu.make_async_copy(ring, ring_s, tab_load).start()
        pltpu.make_async_copy(ring, ring_s, tab_load).wait()

    def plane0():
        plane[z, x] = tables[...]
        tab(0, plane_at(0, 0), x_near[0])
        tab(1, plane_at(0, 0), x_near[1])

    def plane1():
        tab_wait(0, plane_at(0, 3))
        tab(2, plane_at(0, 3), x_near[0])
        tab_wait(1, plane_at(0, 1))

    def plane2():
        tab_wait(2, plane_at(0, 2))
        tab(3, line_at(0), z_near[0])
        tab(4, line_at(0), z_near[1])

    def plane3():
        tab_wait(3, line_at(3))
        tab(5, line_at(3), z_near[0])
        tab_wait(4, line_at(1))

    def plane4():
        tab_wait(5, line_at(2))
        pltpu.make_async_copy(plane, plane_s, tab_load).start()
        pltpu.make_async_copy(plane, plane_s, tab_load).wait()

    def flag0():
        most = jnp.zeros((8, 128), jnp.int32)
        for zz in range(4):
            for xx in range(4):
                most = jnp.maximum(most, plane[zz, xx])
        flags[y, core] = most
        tab(10, flags.at[y, core], sibling)

    def flag1():
        tab_wait(10, flags.at[y, 1 - core])
        tab(11, flags.at[y], y_next)
        tab(12, flags.at[y], y_prev)

    def flag2():
        tab_wait(11, flags.at[lax.rem(y + 3, 4)])
        tab(13, flags.at[lax.rem(y + 3, 4)], y_next)
        tab_wait(12, flags.at[lax.rem(y + 1, 4)])

    def flag3():
        tab_wait(13, flags.at[lax.rem(y + 2, 4)])
        most = jnp.zeros((8, 128), jnp.int32)
        for yy in range(4):
            for cc in range(2):
                most = jnp.maximum(most, flags[yy, cc])
        over[...] = most

    def tab_end():
        for k, ref in enumerate((
            plane_at(0, 0), plane_at(0, 0), plane_at(0, 0), line_at(0), line_at(0), line_at(0), ring.at[0, 0], ring_at(0),
            ring_at(0), ring_at(0), flags.at[0, 0], flags.at[0], flags.at[0], flags.at[0],
        )):
            wait_bytes(ref, tab_send.at[k])

    lane = lax.broadcasted_iota(jnp.int32, (TILE, 128), 1)
    lane_row = lax.broadcasted_iota(jnp.int32, (1, 128), 1)

    def beside(left, right, left_kind, right_kind):
        kinds = jnp.where(lane_row < 64, left_kind, right_kind)
        straight = (kinds & 1).astype(F32)
        turned = (kinds >> 1).astype(F32)
        return (
            jnp.where(lane < 64, left, right) * straight
            + pltpu.roll(jnp.where(lane < 64, right, left), 64, 1) * turned
        )

    def rows_of(c, part=None):
        return pl.ds(c * STEP, STEP) if part is None else pl.ds(c * STEP + part, 1)

    def block(way, dz, dx, rows):
        return whole_amps.at[way, lax.rem(z + dz, 4), lax.rem(x + dx, 4), rows]

    def bundle(way, d, rows):
        if way == 0:
            return whole_amps.at[0, lax.rem(z + d, 4), :, rows]
        return whole_amps.at[1, :, lax.rem(x + d, 4), rows]

    def near(way, d, rows):
        return block(way, 0, d, rows) if way == 0 else block(way, d, 0, rows)

    def step1(c):
        rows = rows_of(c)
        for way in (0, 1):
            for e in (0, 1):
                remote(own.at[way, rows], block(way, 0, 0, rows), amp_send.at[way, 0, e], amp_recv.at[way, 0, e, c], first[way][e])

    def step2(c):
        for way in (0, 1):
            for e in (0, 1):
                d = 3 if e == 0 else 1
                wait_bytes(near(way, d, rows_of(c)), amp_recv.at[way, 0, e, c])
                part = near(way, d, rows_of(c, e))
                remote(part, part, amp_send.at[way, 1, e], amp_recv.at[way, 1, e, c], first[way][e])

    def step3(c):
        for way in (0, 1):
            for e in (0, 1):
                wait_bytes(near(way, 2, rows_of(c, e)), amp_recv.at[way, 1, e, c])
            line = bundle(way, 0, rows_of(c))
            for e in (0, 1):
                remote(line, line, amp_send.at[way, 2, e], amp_recv.at[way, 2, e, c], second[way][e])

    def step4(c):
        for way in (0, 1):
            for e in (0, 1):
                d = 3 if e == 0 else 1
                wait_bytes(bundle(way, d, rows_of(c)), amp_recv.at[way, 2, e, c])
                part = bundle(way, d, rows_of(c, e))
                remote(part, part, amp_send.at[way, 3, e], amp_recv.at[way, 3, e, c], second[way][e])

    def step5(c):
        for way in (0, 1):
            for e in (0, 1):
                wait_bytes(bundle(way, 2, rows_of(c, e)), amp_recv.at[way, 3, e, c])

    def tick(t):
        for lead, step in ((8, step1), (6, step2), (4, step3), (2, step4)):
            c = t + lead
            pl.when((c >= (8 if lead == 8 else 0)) & (c < STEPS))(functools.partial(step, c))

    def fetch(s):
        rows = rows_of(s)
        return pltpu.make_async_copy(whole_amps.at[:, :, :, rows], packed.at[:, :, :, rows], load)

    def arrive(s):
        step5(s)
        fetch(s).start()
        fetch(s).wait()

    def int_rows(p, part=None):
        half = INT_PIECE // 2
        return pl.ds(p * INT_PIECE, INT_PIECE) if part is None else pl.ds(p * INT_PIECE + part * half, half)

    def int_block(dy, dcore, rows):
        return whole_ints.at[lax.rem(y + dy, 4) * 2 + lax.rem(core + dcore, 2), rows]

    def unpack_ints(ref, dy, dcore, half):
        yy, cc = lax.rem(y + dy, 4), lax.rem(core + dcore, 2)

        @pl.loop(0, 8)
        def _(t):
            rows = pl.ds(pl.multiple_of((yy * 2 + cc) * 512 + t * TILE, TILE), TILE)
            for g in range(4):
                one = half * 64 + t * 8 + 2 * g
                two = one + 1
                value = beside(
                    ref[ring_s[yy, cc, 3, one]], ref[ring_s[yy, cc, 3, two]], ring_s[yy, cc, 4, one], ring_s[yy, cc, 4, two]
                )
                top = value.astype(BF16)
                lanes = slice((half * 4 + g) * 128, (half * 4 + g + 1) * 128)
                high[rows, lanes] = top
                low[rows, lanes] = (value - top.astype(F32)).astype(BF16)

    def int_start(p):
        rows = int_rows(p)
        piece, there = own_ints.at[rows], int_block(0, 0, rows)
        remote(piece, there, int_send.at[0], int_recv.at[0, p], y_next)
        remote(piece, there, int_send.at[1], int_recv.at[1, p], y_prev)

    def int_pass(p):
        rows = int_rows(p)
        for e, d, device in ((0, 3, y_next), (1, 1, y_prev)):
            piece = int_block(d, 0, rows)
            wait_bytes(piece, int_recv.at[e, p])
            part = int_block(d, 0, int_rows(p, e))
            remote(part, part, int_send.at[2 + e], int_recv.at[2 + e, p], device)
            remote(piece, piece, sib_send, sib_recv.at[1 + e, p], sibling)

    def int_take(blocks, half):
        first, last = ((0, INT_EARLY), (INT_EARLY, INT_PIECES))[half]

        def enter(i):
            k, dy, dcore = blocks[i]
            if dcore and k == 0:
                wait_bytes(int_block(0, 1, pl.ds(0, INT_PAIRS)), sib_recv.at[0, 0])
            elif dcore:
                @pl.loop(first, last)
                def _(p):
                    wait_bytes(int_block(dy, 1, int_rows(p)), sib_recv.at[k, p])
            pairs = pl.ds(0, INT_PAIRS if half or k == 0 else INT_EARLY * INT_PIECE)
            buffer = (int_a, int_b)[i % 2]
            copy = pltpu.make_async_copy(int_block(dy, dcore, pairs), buffer.at[pairs], int_load.at[i % 2])
            copy.start()
            return copy

        copy = enter(0)
        for i, (k, dy, dcore) in enumerate(blocks):
            copy.wait()
            copy = enter(i + 1) if i + 1 < len(blocks) else None
            unpack_ints((int_a, int_b)[i % 2], dy, dcore, half)
            if k == 0:
                unpack_ints((int_a, int_b)[i % 2], dy, dcore, 1)

    def int_far(p):
        for e in (0, 1):
            wait_bytes(int_block(2, 0, int_rows(p, e)), int_recv.at[2 + e, p])
        piece = int_block(2, 0, int_rows(p))
        remote(piece, piece, sib_send, sib_recv.at[3, p], sibling)

    ring0()
    plane0()

    @pl.loop(0, PAIRS)
    def _(i):
        for way in (0, 1):
            pair = 2 * i + way
            tiles = []
            for place in (2 * pair, 2 * pair + 1):
                both = amps[listing[0, place]]
                tiles.append(both[:, :128] * listing[1, place].astype(F32) + both[:, 128:] * listing[2, place].astype(F32))
            own[way, i] = beside(*tiles, listing[3, 2 * pair], listing[3, 2 * pair + 1])

    for c in range(8):
        step1(c)
    ring1()

    for t in range(8):
        for g in range(8):
            stage[t, g // 2, g % 2] = ints[t * TILE:(t + 1) * TILE, g * 128:(g + 1) * 128]

    @pl.loop(0, INT_PAIRS)
    def _(pair):
        one = 2 * pair
        two = one + 1
        own_ints[pair] = beside(
            stage[listing[4, one], listing[5, one], listing[6, one]], stage[listing[4, two], listing[5, two], listing[6, two]],
            listing[7, one], listing[7, two],
        )

    ring2()

    @pl.loop(0, INT_EARLY)
    def _(p):
        int_start(p)

    remote(own_ints, int_block(0, 0, pl.ds(0, INT_PAIRS)), sib_send, sib_recv.at[0, 0], sibling)
    for way in (0, 1):
        pltpu.make_async_copy(own.at[way], whole_amps.at[way, z, x], local.at[way]).start()
    for way in (0, 1):
        pltpu.make_async_copy(own.at[way], whole_amps.at[way, z, x], local.at[way]).wait()

    tick(-6)
    plane1()
    tick(-5)
    tick(-4)
    plane2()
    tick(-3)
    ring3()
    tick(-2)
    unpack_ints(own_ints, 0, 0, 0)
    unpack_ints(own_ints, 0, 0, 1)
    plane3()
    for p in range(2):
        int_pass(p)
    tick(-1)
    int_take([(0, 0, 1)], 0)
    plane4()
    flag0()

    @pl.loop(2, INT_EARLY)
    def _(p):
        int_pass(p)

    @pl.loop(INT_EARLY, INT_PIECES)
    def _(p):
        int_start(p)

    tick(0)
    flag1()
    int_take([(1, 3, 0), (2, 1, 0), (1, 3, 1), (2, 1, 1)], 0)
    tick(1)

    @pl.loop(0, INT_EARLY)
    def _(p):
        int_far(p)

    int_take([(3, 2, 0), (3, 2, 1)], 0)
    tick(2)
    arrive(0)
    arrive(1)

    @pl.loop(INT_EARLY, INT_EARLY + 3)
    def _(p):
        int_pass(p)

    tick(3)

    def stage_wait(slot):
        wait_bytes(stage.at[slot, pl.ds(0, 3)], out_send.at[slot])
        wait_bytes(stage.at[slot, 0], out_self.at[slot])

    def unpack_amps(split, c, zz, xx, at_k):
        for t in (0, 1):
            for g in (0, 1):
                one = (c * 2 + t) * 4 + 2 * g
                two = one + 1
                value = beside(
                    packed[plane_s[zz, xx, 0, one], zz, xx, plane_s[zz, xx, 1, one]],
                    packed[plane_s[zz, xx, 0, two], zz, xx, plane_s[zz, xx, 1, two]],
                    plane_s[zz, xx, 2, one], plane_s[zz, xx, 2, two],
                )
                top = value.astype(BF16)
                lanes = pl.ds(pl.multiple_of(at_k + g * 128, 128), 128)
                split[t * TILE:(t + 1) * TILE, lanes] = top
                split[CHUNK + t * TILE:CHUNK + (t + 1) * TILE, lanes] = (value - top.astype(F32)).astype(BF16)

    @pl.loop(0, 16)
    def _(k):
        unpack_amps(split_a, 0, k // 4, lax.rem(k, 4), k * 256)

    def multiply(unit, c, n, split, split_next, later, parts):
        slot = lax.rem(unit, SLOTS)
        pl.when(unit >= SLOTS)(functools.partial(stage_wait, slot))
        shift = jnp.transpose(jnp.broadcast_to(occ[pl.ds(c, 1), :], (CHUNK, 128)))
        wide = pl.ds(pl.multiple_of(n * WIDE, WIDE), WIDE)
        both = jnp.dot(split[...], high[:, wide], preferred_element_type=F32)
        for zz, xx, at_k in parts:
            unpack_amps(split_next, later, zz, xx, at_k)
        rest = jnp.dot(split[0:CHUNK], low[:, wide], preferred_element_type=F32)
        ladder = both[:CHUNK] + (both[CHUNK:] + rest)
        for q in range(4):
            scaled = ladder[:, q * 128:(q + 1) * 128] / (shift + virt[pl.ds(2 * q + n, 1), :])
            stage[slot, q, 0] = scaled[:TILE]
            stage[slot, q, 1] = scaled[TILE:]

        there = pl.ds(row * (ROWS // TILE) + c * (CHUNK // TILE), CHUNK // TILE)
        for d in (2, 1, 3):
            owner = lax.rem(y + d, 4)
            remote(stage.at[slot, owner], out.at[there], out_send.at[slot], out_recv.at[row], (owner * 2 + n, col))

        @pl.when(core == n)
        def _():
            pltpu.make_async_copy(stage.at[slot, y], out.at[there], out_self.at[slot]).start()

        @pl.when(core != n)
        def _():
            remote(stage.at[slot, y], out.at[there], out_self.at[slot], out_recv.at[row], sibling)

    def after(value, points):
        return sum((value >= p).astype(jnp.int32) for p in points)

    def among(value, points):
        return functools.reduce(lambda a, b: a | b, [value == p for p in points])

    @pl.loop(0, 16)
    def _(k):
        unpack_amps(split_a, 0, k // 4, lax.rem(k, 4), k * 256)

    everything = [(k // 4, k % 4, k * 256) for k in range(16)]

    @pl.loop(0, EARLY)
    def _(i):
        for odd, split, split_next in ((0, split_a, split_b), (1, split_b, split_a)):
            unit = 2 * i + odd
            n = unit // EARLY
            c = unit - n * EARLY

            @pl.when(among(unit, (3, 4, 7, 10)))
            def _():
                tick(4 + after(unit, (4, 7, 10)))

            @pl.when(among(unit, (1, 2, 3, 4, 11)))
            def _():
                arrive(jnp.where(unit == 11, 6, unit + 1))

            later = jnp.where((unit == EARLY - 1), 0, c + 1)
            multiply(unit, c, n, split, split_next, later, everything)
            if odd == 0:
                @pl.when(i == 0)
                def _():
                    int_pass(INT_EARLY + 3)
                    int_pass(INT_EARLY + 4)

                @pl.when(i == 2)
                def _():
                    @pl.loop(INT_EARLY, INT_PIECES)
                    def _(p):
                        int_far(p)
            else:
                @pl.when(i == 0)
                def _():
                    int_pass(INT_EARLY + 5)
                    flag2()

                @pl.when(i == 1)
                def _():
                    int_take([(1, 3, 0), (2, 1, 0), (1, 3, 1), (2, 1, 1)], 1)

                @pl.when(i == 2)
                def _():
                    int_take([(3, 2, 0), (3, 2, 1)], 1)

    @pl.loop(EARLY // 2, CHUNKS // 2)
    def _(i):
        for odd, split, split_next in ((0, split_a, split_b), (1, split_b, split_a)):
            c = 2 * i + odd

            @pl.when(among(c, (6, 8, 9)))
            def _():
                tick(8 + after(c, (8, 9)))

            @pl.when(among(c, (7, 8, 10, 11, 12, 14)))
            def _():
                arrive(7 + after(c, (8, 10, 11, 12, 14)))

            later = jnp.minimum(c + 1, CHUNKS - 1)

            @pl.loop(0, 2)
            def _(n):
                parts = [(n * 2 + k // 4, k % 4, n * 2048 + k * 256) for k in range(8)]
                multiply(2 * c + n, c, n, split, split_next, later, parts)

    flag3()
    for slot in range(SLOTS):
        stage_wait(slot)
    for d in range(1, 8):
        source = lax.rem(row + d, 8)
        wait_bytes(out.at[pl.ds(source * (ROWS // TILE), ROWS // TILE)], out_recv.at[source])
    for way in (0, 1):
        for e in (0, 1):
            wait_bytes(whole_amps.at[way, 0, 0], amp_send.at[way, 0, e])
            wait_bytes(whole_amps.at[way, 0, 0, pl.ds(0, PAIRS // 2)], amp_send.at[way, 1, e])
            wait_bytes(whole_amps.at[way, 0], amp_send.at[way, 2, e])
            wait_bytes(whole_amps.at[way, 0, pl.ds(0, 2)], amp_send.at[way, 3, e])
    for e in (0, 1):
        wait_bytes(whole_ints.at[0], int_send.at[e])
        wait_bytes(whole_ints.at[0, pl.ds(0, INT_PAIRS // 2)], int_send.at[2 + e])
    wait_bytes(whole_ints.at[pl.ds(0, 4)], sib_send)
    tab_end()


def packed_ladder(amplitudes, integrals, tables, listing, occ_shift, virt_shift):
    dma = pltpu.SemaphoreType.DMA
    vmem, anywhere = pl.BlockSpec(memory_space=pltpu.VMEM), pl.BlockSpec(memory_space=pl.ANY)
    out, over, _, _ = pl.pallas_call(
        packed_kernel,
        name="packed_ladder",
        out_shape=(
            jax.ShapeDtypeStruct((8 * ROWS // TILE, TILE, 128), F32),
            jax.ShapeDtypeStruct((8, 128), jnp.int32),
            jax.ShapeDtypeStruct((2, 4, 4, PAIRS, TILE, 128), F32),
            jax.ShapeDtypeStruct((8, INT_PAIRS, TILE, 128), F32),
        ),
        in_specs=[vmem] * 3 + [pl.BlockSpec(memory_space=pltpu.SMEM)] + [vmem] * 2,
        out_specs=(anywhere, vmem, anywhere, anywhere),
        scratch_shapes=[
            pltpu.VMEM((2, PAIRS, TILE, 128), F32),
            pltpu.VMEM((INT_PAIRS, TILE, 128), F32),
            pltpu.VMEM((2, 4, 4, PAIRS, TILE, 128), F32),
            pltpu.VMEM((INT_PAIRS, TILE, 128), F32),
            pltpu.VMEM((INT_PAIRS, TILE, 128), F32),
            pltpu.VMEM((DEPTH, COLS), BF16),
            pltpu.VMEM((DEPTH, COLS), BF16),
            pltpu.VMEM((2 * CHUNK, DEPTH), BF16),
            pltpu.VMEM((2 * CHUNK, DEPTH), BF16),
            pltpu.VMEM((SLOTS, 4, CHUNK // TILE, TILE, 128), F32),
            pltpu.VMEM((4, 4, 8, 128), jnp.int32),
            pltpu.VMEM((4, 2, 8, 128), jnp.int32),
            pltpu.VMEM((4, 2, 8, 128), jnp.int32),
            pltpu.SMEM((4, 4, 8, 128), jnp.int32),
            pltpu.SMEM((4, 2, 8, 128), jnp.int32),
            dma((2, 4, 2)),
            dma((2, 4, 2, STEPS)),
            dma((4,)),
            dma((4, INT_PIECES)),
            dma,
            dma((4, INT_PIECES)),
            dma((14,)),
            dma((14,)),
            dma((SLOTS,)),
            dma((SLOTS,)),
            dma((8,)),
            dma((2,)),
            dma,
            dma((2,)),
            dma,
        ],
        compiler_params=pltpu.CompilerParams(collective_id=0, has_side_effects=True, vmem_limit_bytes=61 << 20),
        cost_estimate=pl.CostEstimate(flops=6 * ROWS * DEPTH * COLS, bytes_accessed=80 << 20, transcendentals=0),
    )(
        amplitudes.reshape(ROWS // TILE, TILE, 256), integrals, tables, listing, occ_shift.reshape(CHUNKS, 128),
        virt_shift.reshape(8, 128),
    )
    return out.reshape(8 * ROWS, 128), over[5, 0]


def shards(amplitudes, integrals, amp_mask, int_mask, occ_shift, virt_shift):
    halves = int_mask.reshape(8, 4, 2, 2).transpose(2, 0, 1, 3)
    masks = jnp.stack([amp_mask.reshape(128), halves.reshape(128)])
    count = jnp.arange(128, dtype=jnp.int32)
    slots = jnp.sum(jnp.where(count[:, None] < count[None, :], masks[:, :, None], 0), axis=1)
    used = slots + masks
    room = jnp.array([STEP_TILES * n for n in NEED], jnp.int32)
    over = jnp.any(used[0].reshape(CHUNKS, 8)[:, 7] > room) | (used[1, 63] > 2 * INT_EARLY * INT_PIECE) | (used[1, 127] > INT_MOST)
    limit = jnp.array([[MOST - 1], [INT_MOST - 1]], jnp.int32)
    at = jnp.where(masks != 0, jnp.minimum(slots, limit), 0)
    kind = jnp.where(masks != 0, 1 + ((at ^ count[None, :]) & 1), 0)
    here = (masks[:, :, None] != 0) & (slots[:, :, None] == count[None, None, :])
    place = jnp.sum(jnp.where(here, count[None, :, None], 0), axis=1)
    turn = 1 + ((place ^ count[None, :]) & 1)
    flags = jnp.broadcast_to(over.astype(jnp.int32), (128,))
    tables = jnp.stack([(at[0] >> 1) & 1, at[0] >> 2, kind[0], at[1] >> 1, kind[1], flags, flags, flags])
    a, b = place
    listing = jnp.stack([
        a >> 2, 1 - ((a >> 1) & 1), (a >> 1) & 1, turn[0], (b >> 3) & 7, (b >> 1) & 3, b >> 6, turn[1]
    ])
    update, over = packed_ladder(amplitudes, integrals, tables, listing, occ_shift, virt_shift)
    return lax.cond(
        over > 0,
        lambda: whole_ladder(amplitudes, integrals, amp_mask, int_mask, occ_shift, virt_shift),
        lambda: update,
    )


def solution(mesh):
    placed = (
        P("row", "col"),
        P("row", "col"),
        P("row", "col"),
        P("row", "col"),
        P("row"),
        P("col"),
    )
    return jax.shard_map(
        shards, mesh=mesh, in_specs=placed, out_specs=P(None, ("col", "row")), check_vma=False
    )
```

```python
import functools

import jax
import jax.numpy as jnp
from jax import lax
from jax.experimental import pallas as pl
from jax.experimental.pallas import tpu as pltpu
from jax.sharding import PartitionSpec as P

MESH = pl.DeviceIdType.MESH
F32, BF16 = jnp.float32, jnp.bfloat16
TILE = 64
ROWS, DEPTH, COLS = 2048, 4096, 1024
CHUNK = 128
CHUNKS = ROWS // CHUNK
HALF = CHUNK // 2
PIECE = 64
PIECES = 512 // PIECE
AHEAD = 5
CATCH = 2 * AHEAD
WIDE = 512


def wait_bytes(ref, sem):
    pltpu.make_async_copy(ref, ref, sem).wait()


def whole_kernel(
    amps, ints, amp_gain, int_gain, occ, virt,
    out, whole_amps,
    own, whole_ints, high, low, chunk_in, split, stage,
    amp_send, amp_recv, int_send, int_recv, sib_send, sib_recv, out_send, out_recv, local, load,
):
    row, col = lax.axis_index("row"), lax.axis_index("col")
    y, core = row // 2, row % 2
    z, x = col // 4, col % 4

    def at(dy=0, dz=0, dx=0, dcore=0):
        r = lax.rem(y + dy, 4) * 2 + lax.rem(core + dcore, 2)
        return r, lax.rem(z + dz, 4) * 4 + lax.rem(x + dx, 4)

    sibling = at(dcore=1)
    y_next, y_prev = at(dy=1), at(dy=3)
    x_near = (at(dx=1), at(dx=3))
    z_near = (at(dz=1), at(dz=3))
    first, second = (x_near, z_near), (z_near, x_near)
    partners = [*x_near, *z_near, sibling] + [at(dy=d, dcore=c) for d in (1, 2, 3) for c in (0, 1)]

    barrier = pltpu.get_barrier_semaphore()
    for partner in partners:
        pl.semaphore_signal(barrier, inc=1, device_id=partner, device_id_type=MESH)
    pl.semaphore_wait(barrier, len(partners))

    def remote(src, dst, send, recv, device):
        pltpu.make_async_remote_copy(
            src_ref=src, dst_ref=dst, send_sem=send, recv_sem=recv, device_id=device, device_id_type=MESH
        ).start()

    def rows_of(c, part=None):
        if part is None:
            return pl.ds(pl.multiple_of(c * CHUNK, CHUNK), CHUNK)
        return pl.ds(pl.multiple_of(c * CHUNK + part * HALF, HALF), HALF)

    def block(way, dz, dx, rows):
        return whole_amps.at[way, lax.rem(z + dz, 4), lax.rem(x + dx, 4), rows, :]

    def bundle(way, d, rows):
        if way == 0:
            return whole_amps.at[0, lax.rem(z + d, 4), :, rows, :]
        return whole_amps.at[1, :, lax.rem(x + d, 4), rows, :]

    def near(way, d, rows):
        return block(way, 0, d, rows) if way == 0 else block(way, d, 0, rows)

    def step1(c):
        rows = rows_of(c)
        for way in (0, 1):
            for e in (0, 1):
                remote(own.at[way, rows, :], block(way, 0, 0, rows), amp_send.at[way, 0, e], amp_recv.at[way, 0, e, c], first[way][e])

    def step2(c):
        for way in (0, 1):
            for e in (0, 1):
                d = 3 if e == 0 else 1
                wait_bytes(near(way, d, rows_of(c)), amp_recv.at[way, 0, e, c])
                part = near(way, d, rows_of(c, e))
                remote(part, part, amp_send.at[way, 1, e], amp_recv.at[way, 1, e, c], first[way][e])

    def step3(c):
        for way in (0, 1):
            for e in (0, 1):
                wait_bytes(near(way, 2, rows_of(c, e)), amp_recv.at[way, 1, e, c])
            line = bundle(way, 0, rows_of(c))
            for e in (0, 1):
                remote(line, line, amp_send.at[way, 2, e], amp_recv.at[way, 2, e, c], second[way][e])

    def step4(c):
        for way in (0, 1):
            for e in (0, 1):
                d = 3 if e == 0 else 1
                wait_bytes(bundle(way, d, rows_of(c)), amp_recv.at[way, 2, e, c])
                part = bundle(way, d, rows_of(c, e))
                remote(part, part, amp_send.at[way, 3, e], amp_recv.at[way, 3, e, c], second[way][e])

    def step5(c):
        for way in (0, 1):
            for e in (0, 1):
                wait_bytes(bundle(way, 2, rows_of(c, e)), amp_recv.at[way, 3, e, c])

    def tick(t):
        for lead, step in ((4, step1), (3, step2), (2, step3), (1, step4), (0, step5)):
            c = t + lead
            pl.when((c >= (4 if lead == 4 else 0)) & (c < CHUNKS))(functools.partial(step, c))

    def int_rows(p, part=None):
        if part is None:
            return pl.ds(pl.multiple_of(p * PIECE, PIECE), PIECE)
        return pl.ds(pl.multiple_of(p * PIECE + part * (PIECE // 2), PIECE // 2), PIECE // 2)

    def int_block(dy, dcore, rows):
        return whole_ints.at[lax.rem(y + dy, 4) * 2 + lax.rem(core + dcore, 2), rows, :]

    def halve(dy, dcore, rows_at, count):
        b = lax.rem(y + dy, 4) * 2 + lax.rem(core + dcore, 2)
        value = whole_ints[b, pl.ds(rows_at, count), :]
        top = value.astype(BF16)
        rows = pl.ds(pl.multiple_of(b * 512 + rows_at, count), count)
        high[rows, :] = top
        low[rows, :] = (value - top.astype(F32)).astype(BF16)

    def int_start(p):
        rows = int_rows(p)
        piece = int_block(0, 0, rows)
        remote(piece, piece, int_send.at[0], int_recv.at[0, p], y_next)
        remote(piece, piece, int_send.at[1], int_recv.at[1, p], y_prev)
        remote(piece, piece, sib_send, sib_recv.at[0, p], sibling)

    def int_pass(p):
        rows = int_rows(p)
        for e, d, device in ((0, 3, y_next), (1, 1, y_prev)):
            piece = int_block(d, 0, rows)
            wait_bytes(piece, int_recv.at[e, p])
            part = int_block(d, 0, int_rows(p, e))
            remote(part, part, int_send.at[2 + e], int_recv.at[2 + e, p], device)
            remote(piece, piece, sib_send, sib_recv.at[1 + e, p], sibling)

    def int_near(p):
        base = pl.multiple_of(p * PIECE, PIECE)
        halve(0, 0, base, PIECE)
        halve(3, 0, base, PIECE)
        halve(1, 0, base, PIECE)

    def int_sibling(p):
        rows, base = int_rows(p), pl.multiple_of(p * PIECE, PIECE)
        for k, d in ((0, 0), (1, 3), (2, 1)):
            wait_bytes(int_block(d, 1, rows), sib_recv.at[k, p])
            halve(d, 1, base, PIECE)

    def int_far(p):
        rows, base = int_rows(p), pl.multiple_of(p * PIECE, PIECE)
        for e in (0, 1):
            wait_bytes(int_block(2, 0, int_rows(p, e)), int_recv.at[2 + e, p])
        piece = int_block(2, 0, rows)
        remote(piece, piece, sib_send, sib_recv.at[3, p], sibling)
        halve(2, 0, base, PIECE)

    def int_far_sibling(p):
        wait_bytes(int_block(2, 1, int_rows(p)), sib_recv.at[3, p])
        halve(2, 1, pl.multiple_of(p * PIECE, PIECE), PIECE)

    def mask_chunk(c):
        for k in range(CHUNK // TILE):
            rows = pl.ds(pl.multiple_of(c * CHUNK + k * TILE, TILE), TILE)
            gain = amp_gain[pl.ds(c * (CHUNK // TILE) + k, 1), :]
            value = amps[rows, :] * gain
            own[0, rows, :] = value[:, :128]
            own[1, rows, :] = value[:, 128:]

    for c in range(4):
        mask_chunk(c)
        step1(c)

    @pl.loop(0, PIECES)
    def _(p):
        rows = int_rows(p)
        whole_ints[row, rows, :] = ints[rows, :] * int_gain[pl.ds(p, 1), :]
        int_start(p)

    @pl.loop(4, CHUNKS)
    def _(c):
        mask_chunk(c)

    for way in (0, 1):
        pltpu.make_async_copy(own.at[way], whole_amps.at[way, z, x], local.at[way]).start()
    for way in (0, 1):
        pltpu.make_async_copy(own.at[way], whole_amps.at[way, z, x], local.at[way]).wait()

    @pl.loop(0, 3)
    def _(t):
        tick(t - 3)

    @pl.loop(0, AHEAD - 1)
    def _(t):
        tick(t)
        for q in (0, 1):
            int_pass(2 * t + q)
        for q in (0, 1):
            int_near(2 * t + q)

        @pl.when(t > 0)
        def _():
            for q in (0, 1):
                int_sibling(2 * t - 2 + q)

    tick(AHEAD - 1)
    for q in (0, 1):
        int_sibling(2 * (AHEAD - 2) + q)

    @pl.loop(0, PIECES // 2)
    def _(p):
        int_far(p)

    tick(AHEAD)

    @pl.loop(PIECES // 2, PIECES)
    def _(p):
        int_far(p)
        int_far_sibling(p - PIECES // 2)

    @pl.loop(PIECES // 2, PIECES)
    def _(p):
        int_far_sibling(p)

    def fetch(c):
        slot = lax.rem(c, 2)
        return pltpu.make_async_copy(whole_amps.at[:, :, :, rows_of(c), :], chunk_in.at[slot], load.at[slot])

    @pl.loop(0, CHUNKS)
    def _(c):
        @pl.when((c > 0) & ((c >= CATCH) | (lax.rem(c, 2) == 0)))
        def _():
            tick(jnp.where(c < CATCH, AHEAD + c // 2, c))

        @pl.when((c == 0) | (c >= CATCH))
        def _():
            fetch(c).start()

        fetch(c).wait()

        @pl.when(c < CATCH - 1)
        def _():
            fetch(c + 1).start()

        slot = lax.rem(c, 2)

        @pl.loop(0, 16)
        def _(k):
            value = jnp.concatenate([chunk_in[slot, 0, k // 4, lax.rem(k, 4)], chunk_in[slot, 1, k // 4, lax.rem(k, 4)]], axis=1)
            top = value.astype(BF16)
            at_k = pl.ds(pl.multiple_of(k * 256, 256), 256)
            split[pl.ds(0, CHUNK), at_k] = top
            split[pl.ds(CHUNK, CHUNK), at_k] = (value - top.astype(F32)).astype(BF16)

        rows = rows_of(c)

        @pl.loop(0, COLS // WIDE)
        def _(n):
            wide = pl.ds(pl.multiple_of(n * WIDE, WIDE), WIDE)
            both = jnp.dot(split[...], high[:, wide], preferred_element_type=F32)
            rest = jnp.dot(split[pl.ds(0, CHUNK)], low[:, wide], preferred_element_type=F32)
            scaled = (both[:CHUNK] + (both[CHUNK:] + rest)) / (occ[rows, :] + virt[:, wide])
            for q in range(WIDE // 128):
                stage[n * (WIDE // 128) + q, rows, :] = scaled[:, q * 128:(q + 1) * 128]

        there = pl.ds(pl.multiple_of(row * ROWS + c * CHUNK, CHUNK), CHUNK)
        for d in (4, 5, 2, 3, 6, 7, 1):
            owner = lax.rem(row + d, 8)
            remote(stage.at[owner, rows, :], out.at[there, :], out_send, out_recv.at[row], (owner, col))
        pltpu.make_async_copy(stage.at[row, rows, :], out.at[there, :], out_recv.at[row]).start()

    for source in range(8):
        wait_bytes(out.at[pl.ds(source * ROWS, ROWS), :], out_recv.at[source])
    wait_bytes(stage.at[pl.ds(0, 7)], out_send)
    for way in (0, 1):
        for e in (0, 1):
            wait_bytes(whole_amps.at[way, 0, 0], amp_send.at[way, 0, e])
            wait_bytes(whole_amps.at[way, 0, 0, pl.ds(0, ROWS // 2)], amp_send.at[way, 1, e])
            wait_bytes(whole_amps.at[way, 0], amp_send.at[way, 2, e])
            wait_bytes(whole_amps.at[way, 0, pl.ds(0, 2)], amp_send.at[way, 3, e])
    for e in (0, 1):
        wait_bytes(whole_ints.at[0], int_send.at[e])
        wait_bytes(whole_ints.at[0, pl.ds(0, 256)], int_send.at[2 + e])
    wait_bytes(whole_ints.at[pl.ds(0, 4)], sib_send)


def whole_ladder(amplitudes, integrals, amp_mask, int_mask, occ_shift, virt_shift):
    amp_gain = jnp.repeat(amp_mask.astype(F32), TILE, axis=1)
    int_gain = jnp.repeat(int_mask.astype(F32), TILE, axis=1)
    dma = pltpu.SemaphoreType.DMA
    vmem, anywhere = pl.BlockSpec(memory_space=pltpu.VMEM), pl.BlockSpec(memory_space=pl.ANY)
    out, _ = pl.pallas_call(
        whole_kernel,
        name="whole_ladder",
        out_shape=(
            jax.ShapeDtypeStruct((8 * ROWS, 128), F32),
            jax.ShapeDtypeStruct((2, 4, 4, ROWS, 128), F32),
        ),
        in_specs=[vmem] * 6,
        out_specs=(anywhere, anywhere),
        scratch_shapes=[
            pltpu.VMEM((2, ROWS, 128), F32),
            pltpu.VMEM((8, 512, COLS), F32),
            pltpu.VMEM((DEPTH, COLS), BF16),
            pltpu.VMEM((DEPTH, COLS), BF16),
            pltpu.VMEM((2, 2, 4, 4, CHUNK, 128), F32),
            pltpu.VMEM((2 * CHUNK, DEPTH), BF16),
            pltpu.VMEM((8, ROWS, 128), F32),
            dma((2, 4, 2)),
            dma((2, 4, 2, CHUNKS)),
            dma((4,)),
            dma((4, PIECES)),
            dma,
            dma((4, PIECES)),
            dma,
            dma((8,)),
            dma((2,)),
            dma((2,)),
        ],
        compiler_params=pltpu.CompilerParams(collective_id=1, has_side_effects=True, vmem_limit_bytes=60 << 20),
        cost_estimate=pl.CostEstimate(flops=6 * ROWS * DEPTH * COLS, bytes_accessed=80 << 20, transcendentals=0),
    )(amplitudes, integrals, amp_gain, int_gain, occ_shift[:, None], virt_shift[None, :])
    return out


MOST = 104
PAIRS = MOST // 4
STEPS = 13
STEP = PAIRS // STEPS
STEP_TILES = MOST // STEPS
NEED = (1, 2, 3, 4, 5, 6, 7, 7, 8, 9, 9, 10, 11, 12, 12, 13)
INT_MOST = 104
INT_PAIRS = INT_MOST // 2
INT_PIECES = 13
INT_PIECE = INT_PAIRS // INT_PIECES
INT_EARLY = 7
SLOTS = 8
EARLY = 4


def packed_kernel(
    amps, ints, tables, listing, occ, virt,
    out, over, whole_amps, whole_ints,
    own, own_ints, packed, int_a, int_b, high, low, split_a, split_b, stage, plane, ring, flags, plane_s, ring_s,
    amp_send, amp_recv, int_send, int_recv, sib_send, sib_recv, tab_send, tab_recv, out_send, out_self, out_recv, local, load,
    int_load, tab_load,
):
    row, col = lax.axis_index("row"), lax.axis_index("col")
    y, core = row // 2, row % 2
    z, x = col // 4, col % 4

    def at(dy=0, dz=0, dx=0, dcore=0):
        r = lax.rem(y + dy, 4) * 2 + lax.rem(core + dcore, 2)
        return r, lax.rem(z + dz, 4) * 4 + lax.rem(x + dx, 4)

    sibling = at(dcore=1)
    y_next, y_prev = at(dy=1), at(dy=3)
    x_near = (at(dx=1), at(dx=3))
    z_near = (at(dz=1), at(dz=3))
    first, second = (x_near, z_near), (z_near, x_near)
    partners = [*x_near, *z_near, sibling] + [at(dy=d, dcore=c) for d in (1, 2, 3) for c in (0, 1)]

    barrier = pltpu.get_barrier_semaphore()
    for partner in partners:
        pl.semaphore_signal(barrier, inc=1, device_id=partner, device_id_type=MESH)
    pl.semaphore_wait(barrier, len(partners))

    def remote(src, dst, send, recv, device):
        pltpu.make_async_remote_copy(
            src_ref=src, dst_ref=dst, send_sem=send, recv_sem=recv, device_id=device, device_id_type=MESH
        ).start()

    def plane_at(dz, dx):
        return plane.at[lax.rem(z + dz, 4), lax.rem(x + dx, 4)]

    def line_at(dz):
        return plane.at[lax.rem(z + dz, 4)]

    def ring_at(dy):
        return ring.at[lax.rem(y + dy, 4)]

    def tab(k, ref, device):
        remote(ref, ref, tab_send.at[k], tab_recv.at[k], device)

    def tab_wait(k, ref):
        wait_bytes(ref, tab_recv.at[k])

    def ring0():
        ring[y, core] = tables[...]
        tab(6, ring.at[y, core], sibling)

    def ring1():
        tab_wait(6, ring.at[y, 1 - core])
        tab(7, ring_at(0), y_next)
        tab(8, ring_at(0), y_prev)

    def ring2():
        tab_wait(7, ring_at(3))
        tab(9, ring_at(3), y_next)
        tab_wait(8, ring_at(1))

    def ring3():
        tab_wait(9, ring_at(2))
        pltpu.make_async_copy(ring, ring_s, tab_load).start()
        pltpu.make_async_copy(ring, ring_s, tab_load).wait()

    def plane0():
        plane[z, x] = tables[...]
        tab(0, plane_at(0, 0), x_near[0])
        tab(1, plane_at(0, 0), x_near[1])

    def plane1():
        tab_wait(0, plane_at(0, 3))
        tab(2, plane_at(0, 3), x_near[0])
        tab_wait(1, plane_at(0, 1))

    def plane2():
        tab_wait(2, plane_at(0, 2))
        tab(3, line_at(0), z_near[0])
        tab(4, line_at(0), z_near[1])

    def plane3():
        tab_wait(3, line_at(3))
        tab(5, line_at(3), z_near[0])
        tab_wait(4, line_at(1))

    def plane4():
        tab_wait(5, line_at(2))
        pltpu.make_async_copy(plane, plane_s, tab_load).start()
        pltpu.make_async_copy(plane, plane_s, tab_load).wait()

    def flag0():
        most = jnp.zeros((8, 128), jnp.int32)
        for zz in range(4):
            for xx in range(4):
                most = jnp.maximum(most, plane[zz, xx])
        flags[y, core] = most
        tab(10, flags.at[y, core], sibling)

    def flag1():
        tab_wait(10, flags.at[y, 1 - core])
        tab(11, flags.at[y], y_next)
        tab(12, flags.at[y], y_prev)

    def flag2():
        tab_wait(11, flags.at[lax.rem(y + 3, 4)])
        tab(13, flags.at[lax.rem(y + 3, 4)], y_next)
        tab_wait(12, flags.at[lax.rem(y + 1, 4)])

    def flag3():
        tab_wait(13, flags.at[lax.rem(y + 2, 4)])
        most = jnp.zeros((8, 128), jnp.int32)
        for yy in range(4):
            for cc in range(2):
                most = jnp.maximum(most, flags[yy, cc])
        over[...] = most

    def tab_end():
        for k, ref in enumerate((
            plane_at(0, 0), plane_at(0, 0), plane_at(0, 0), line_at(0), line_at(0), line_at(0), ring.at[0, 0], ring_at(0),
            ring_at(0), ring_at(0), flags.at[0, 0], flags.at[0], flags.at[0], flags.at[0],
        )):
            wait_bytes(ref, tab_send.at[k])

    lane = lax.broadcasted_iota(jnp.int32, (TILE, 128), 1)
    lane_row = lax.broadcasted_iota(jnp.int32, (1, 128), 1)

    def beside(left, right, left_kind, right_kind):
        kinds = jnp.where(lane_row < 64, left_kind, right_kind)
        straight = (kinds & 1).astype(F32)
        turned = (kinds >> 1).astype(F32)
        return (
            jnp.where(lane < 64, left, right) * straight
            + pltpu.roll(jnp.where(lane < 64, right, left), 64, 1) * turned
        )

    def rows_of(c, part=None):
        return pl.ds(c * STEP, STEP) if part is None else pl.ds(c * STEP + part, 1)

    def block(way, dz, dx, rows):
        return whole_amps.at[way, lax.rem(z + dz, 4), lax.rem(x + dx, 4), rows]

    def bundle(way, d, rows):
        if way == 0:
            return whole_amps.at[0, lax.rem(z + d, 4), :, rows]
        return whole_amps.at[1, :, lax.rem(x + d, 4), rows]

    def near(way, d, rows):
        return block(way, 0, d, rows) if way == 0 else block(way, d, 0, rows)

    def step1(c):
        rows = rows_of(c)
        for way in (0, 1):
            for e in (0, 1):
                remote(own.at[way, rows], block(way, 0, 0, rows), amp_send.at[way, 0, e], amp_recv.at[way, 0, e, c], first[way][e])

    def step2(c):
        for way in (0, 1):
            for e in (0, 1):
                d = 3 if e == 0 else 1
                wait_bytes(near(way, d, rows_of(c)), amp_recv.at[way, 0, e, c])
                part = near(way, d, rows_of(c, e))
                remote(part, part, amp_send.at[way, 1, e], amp_recv.at[way, 1, e, c], first[way][e])

    def step3(c):
        for way in (0, 1):
            for e in (0, 1):
                wait_bytes(near(way, 2, rows_of(c, e)), amp_recv.at[way, 1, e, c])
            line = bundle(way, 0, rows_of(c))
            for e in (0, 1):
                remote(line, line, amp_send.at[way, 2, e], amp_recv.at[way, 2, e, c], second[way][e])

    def step4(c):
        for way in (0, 1):
            for e in (0, 1):
                d = 3 if e == 0 else 1
                wait_bytes(bundle(way, d, rows_of(c)), amp_recv.at[way, 2, e, c])
                part = bundle(way, d, rows_of(c, e))
                remote(part, part, amp_send.at[way, 3, e], amp_recv.at[way, 3, e, c], second[way][e])

    def step5(c):
        for way in (0, 1):
            for e in (0, 1):
                wait_bytes(bundle(way, 2, rows_of(c, e)), amp_recv.at[way, 3, e, c])

    def tick(t, leads=(2, 4, 6, 8)):
        for lead, step in zip(leads, (step4, step3, step2, step1)):
            c = t + lead
            pl.when((c >= 0) & (c < STEPS))(functools.partial(step, c))

    def brisk(t):
        tick(t, (1, 2, 3, 5 if t >= 0 else STEPS + 3))

    def fetch(s):
        rows = rows_of(s)
        return pltpu.make_async_copy(whole_amps.at[:, :, :, rows], packed.at[:, :, :, rows], load)

    def arrive(s):
        step5(s)
        fetch(s).start()
        fetch(s).wait()

    def int_rows(p, part=None):
        half = INT_PIECE // 2
        return pl.ds(p * INT_PIECE, INT_PIECE) if part is None else pl.ds(p * INT_PIECE + part * half, half)

    def int_block(dy, dcore, rows):
        return whole_ints.at[lax.rem(y + dy, 4) * 2 + lax.rem(core + dcore, 2), rows]

    def unpack_ints(ref, dy, dcore, half):
        yy, cc = lax.rem(y + dy, 4), lax.rem(core + dcore, 2)

        @pl.loop(0, 8)
        def _(t):
            rows = pl.ds(pl.multiple_of((yy * 2 + cc) * 512 + t * TILE, TILE), TILE)
            for g in range(4):
                one = half * 64 + t * 8 + 2 * g
                two = one + 1
                value = beside(
                    ref[ring_s[yy, cc, 3, one]], ref[ring_s[yy, cc, 3, two]], ring_s[yy, cc, 4, one], ring_s[yy, cc, 4, two]
                )
                top = value.astype(BF16)
                lanes = slice((half * 4 + g) * 128, (half * 4 + g + 1) * 128)
                high[rows, lanes] = top
                low[rows, lanes] = (value - top.astype(F32)).astype(BF16)

    def int_start(p):
        rows = int_rows(p)
        piece, there = own_ints.at[rows], int_block(0, 0, rows)
        remote(piece, there, int_send.at[0], int_recv.at[0, p], y_next)
        remote(piece, there, int_send.at[1], int_recv.at[1, p], y_prev)

    def int_pass(p):
        rows = int_rows(p)
        for e, d, device in ((0, 3, y_next), (1, 1, y_prev)):
            piece = int_block(d, 0, rows)
            wait_bytes(piece, int_recv.at[e, p])
            part = int_block(d, 0, int_rows(p, e))
            remote(part, part, int_send.at[2 + e], int_recv.at[2 + e, p], device)
            remote(piece, piece, sib_send, sib_recv.at[1 + e, p], sibling)

    def int_take(blocks, half):
        first, last = ((0, INT_EARLY), (INT_EARLY, INT_PIECES))[half]

        def enter(i):
            k, dy, dcore = blocks[i]
            if dcore and k == 0:
                wait_bytes(int_block(0, 1, pl.ds(0, INT_PAIRS)), sib_recv.at[0, 0])
            elif dcore:
                @pl.loop(first, last)
                def _(p):
                    wait_bytes(int_block(dy, 1, int_rows(p)), sib_recv.at[k, p])
            pairs = pl.ds(0, INT_PAIRS if half or k == 0 else INT_EARLY * INT_PIECE)
            buffer = (int_a, int_b)[i % 2]
            copy = pltpu.make_async_copy(int_block(dy, dcore, pairs), buffer.at[pairs], int_load.at[i % 2])
            copy.start()
            return copy

        copy = enter(0)
        for i, (k, dy, dcore) in enumerate(blocks):
            copy.wait()
            copy = enter(i + 1) if i + 1 < len(blocks) else None
            unpack_ints((int_a, int_b)[i % 2], dy, dcore, half)
            if k == 0:
                unpack_ints((int_a, int_b)[i % 2], dy, dcore, 1)

    def int_far(p):
        for e in (0, 1):
            wait_bytes(int_block(2, 0, int_rows(p, e)), int_recv.at[2 + e, p])
        piece = int_block(2, 0, int_rows(p))
        remote(piece, piece, sib_send, sib_recv.at[3, p], sibling)

    ring0()
    plane0()

    @pl.loop(0, PAIRS)
    def _(i):
        for way in (0, 1):
            pair = 2 * i + way
            tiles = []
            for place in (2 * pair, 2 * pair + 1):
                both = amps[listing[0, place]]
                tiles.append(both[:, :128] * listing[1, place].astype(F32) + both[:, 128:] * listing[2, place].astype(F32))
            own[way, i] = beside(*tiles, listing[3, 2 * pair], listing[3, 2 * pair + 1])

    for c in range(5):
        step1(c)
    ring1()

    for t in range(8):
        for g in range(8):
            stage[t, g // 2, g % 2] = ints[t * TILE:(t + 1) * TILE, g * 128:(g + 1) * 128]

    @pl.loop(0, INT_PAIRS)
    def _(pair):
        one = 2 * pair
        two = one + 1
        own_ints[pair] = beside(
            stage[listing[4, one], listing[5, one], listing[6, one]], stage[listing[4, two], listing[5, two], listing[6, two]],
            listing[7, one], listing[7, two],
        )

    ring2()

    @pl.loop(0, INT_EARLY)
    def _(p):
        int_start(p)

    remote(own_ints, int_block(0, 0, pl.ds(0, INT_PAIRS)), sib_send, sib_recv.at[0, 0], sibling)
    for way in (0, 1):
        pltpu.make_async_copy(own.at[way], whole_amps.at[way, z, x], local.at[way]).start()
    for way in (0, 1):
        pltpu.make_async_copy(own.at[way], whole_amps.at[way, z, x], local.at[way]).wait()

    brisk(-3)
    plane1()
    ring3()
    unpack_ints(own_ints, 0, 0, 0)
    brisk(-2)
    plane2()
    unpack_ints(own_ints, 0, 0, 1)
    int_pass(0)
    int_pass(1)
    int_take([(0, 0, 1)], 0)
    brisk(-1)
    plane3()

    @pl.loop(2, INT_EARLY)
    def _(p):
        int_pass(p)

    @pl.loop(INT_EARLY, INT_PIECES)
    def _(p):
        int_start(p)

    brisk(0)
    plane4()
    flag0()
    int_take([(1, 3, 0), (2, 1, 0), (1, 3, 1), (2, 1, 1)], 0)

    @pl.loop(0, INT_EARLY)
    def _(p):
        int_far(p)

    brisk(1)
    flag1()
    int_take([(3, 2, 0), (3, 2, 1)], 0)
    arrive(0)
    arrive(1)

    @pl.loop(INT_EARLY, INT_EARLY + 2)
    def _(p):
        int_pass(p)

    step2(5)
    step1(7)
    step1(8)

    def stage_wait(slot):
        wait_bytes(stage.at[slot, pl.ds(0, 3)], out_send.at[slot])
        wait_bytes(stage.at[slot, 0], out_self.at[slot])

    def unpack_amps(split, c, zz, xx, at_k):
        for t in (0, 1):
            for g in (0, 1):
                one = (c * 2 + t) * 4 + 2 * g
                two = one + 1
                value = beside(
                    packed[plane_s[zz, xx, 0, one], zz, xx, plane_s[zz, xx, 1, one]],
                    packed[plane_s[zz, xx, 0, two], zz, xx, plane_s[zz, xx, 1, two]],
                    plane_s[zz, xx, 2, one], plane_s[zz, xx, 2, two],
                )
                top = value.astype(BF16)
                lanes = pl.ds(pl.multiple_of(at_k + g * 128, 128), 128)
                split[t * TILE:(t + 1) * TILE, lanes] = top
                split[CHUNK + t * TILE:CHUNK + (t + 1) * TILE, lanes] = (value - top.astype(F32)).astype(BF16)

    @pl.loop(0, 16)
    def _(k):
        unpack_amps(split_a, 0, k // 4, lax.rem(k, 4), k * 256)

    def multiply(unit, c, n, split, split_next, later, parts):
        slot = lax.rem(unit, SLOTS)
        pl.when(unit >= SLOTS)(functools.partial(stage_wait, slot))
        shift = jnp.transpose(jnp.broadcast_to(occ[pl.ds(c, 1), :], (CHUNK, 128)))
        wide = pl.ds(pl.multiple_of(n * WIDE, WIDE), WIDE)
        both = jnp.dot(split[...], high[:, wide], preferred_element_type=F32)
        for zz, xx, at_k in parts:
            unpack_amps(split_next, later, zz, xx, at_k)
        rest = jnp.dot(split[0:CHUNK], low[:, wide], preferred_element_type=F32)
        ladder = both[:CHUNK] + (both[CHUNK:] + rest)
        for q in range(4):
            scaled = ladder[:, q * 128:(q + 1) * 128] / (shift + virt[pl.ds(2 * q + n, 1), :])
            stage[slot, q, 0] = scaled[:TILE]
            stage[slot, q, 1] = scaled[TILE:]

        there = pl.ds(row * (ROWS // TILE) + c * (CHUNK // TILE), CHUNK // TILE)
        for d in (2, 1, 3):
            owner = lax.rem(y + d, 4)
            remote(stage.at[slot, owner], out.at[there], out_send.at[slot], out_recv.at[row], (owner * 2 + n, col))

        @pl.when(core == n)
        def _():
            pltpu.make_async_copy(stage.at[slot, y], out.at[there], out_self.at[slot]).start()

        @pl.when(core != n)
        def _():
            remote(stage.at[slot, y], out.at[there], out_self.at[slot], out_recv.at[row], sibling)

    def after(value, points):
        return sum((value >= p).astype(jnp.int32) for p in points)

    def among(value, points):
        return functools.reduce(lambda a, b: a | b, [value == p for p in points])

    @pl.loop(0, 16)
    def _(k):
        unpack_amps(split_a, 0, k // 4, lax.rem(k, 4), k * 256)

    everything = [(k // 4, k % 4, k * 256) for k in range(16)]

    @pl.loop(0, EARLY)
    def _(i):
        for odd, split, split_next in ((0, split_a, split_b), (1, split_b, split_a)):
            unit = 2 * i + odd
            n = unit // EARLY
            c = unit - n * EARLY

            @pl.when(among(unit, (1, 2, 4, 6)))
            def _():
                tick(1 + after(unit, (2, 4, 6)))

            @pl.when(among(unit, (1, 2, 5, 7)))
            def _():
                arrive(2 + after(unit, (2, 5, 7)))

            later = jnp.where((unit == EARLY - 1), 0, c + 1)
            multiply(unit, c, n, split, split_next, later, everything)
            if odd == 0:
                @pl.when(i == 0)
                def _():
                    int_pass(INT_EARLY + 2)
                    int_pass(INT_EARLY + 3)
                    step3(4)
                    step2(6)
            else:
                @pl.when(i == 0)
                def _():
                    int_pass(INT_EARLY + 4)
                    int_pass(INT_EARLY + 5)
                    flag2()
                    int_take([(1, 3, 0), (2, 1, 0), (1, 3, 1), (2, 1, 1)], 1)

                @pl.when(i == 1)
                def _():
                    @pl.loop(INT_EARLY, INT_PIECES)
                    def _(p):
                        int_far(p)

                    int_take([(3, 2, 0), (3, 2, 1)], 1)

    @pl.loop(EARLY // 2, CHUNKS // 2)
    def _(i):
        for odd, split, split_next in ((0, split_a, split_b), (1, split_b, split_a)):
            c = 2 * i + odd

            @pl.when(among(c, (5, 6, 8, 10, 11, 13)))
            def _():
                tick(5 + after(c, (6, 8, 10, 11, 13)))

            @pl.when(among(c, (5, 7, 8, 10, 11, 12, 14)))
            def _():
                arrive(6 + after(c, (7, 8, 10, 11, 12, 14)))

            later = jnp.minimum(c + 1, CHUNKS - 1)

            @pl.loop(0, 2)
            def _(n):
                parts = [(n * 2 + k // 4, k % 4, n * 2048 + k * 256) for k in range(8)]
                multiply(2 * c + n, c, n, split, split_next, later, parts)

    flag3()
    for slot in range(SLOTS):
        stage_wait(slot)
    for d in range(1, 8):
        source = lax.rem(row + d, 8)
        wait_bytes(out.at[pl.ds(source * (ROWS // TILE), ROWS // TILE)], out_recv.at[source])
    for way in (0, 1):
        for e in (0, 1):
            wait_bytes(whole_amps.at[way, 0, 0], amp_send.at[way, 0, e])
            wait_bytes(whole_amps.at[way, 0, 0, pl.ds(0, PAIRS // 2)], amp_send.at[way, 1, e])
            wait_bytes(whole_amps.at[way, 0], amp_send.at[way, 2, e])
            wait_bytes(whole_amps.at[way, 0, pl.ds(0, 2)], amp_send.at[way, 3, e])
    for e in (0, 1):
        wait_bytes(whole_ints.at[0], int_send.at[e])
        wait_bytes(whole_ints.at[0, pl.ds(0, INT_PAIRS // 2)], int_send.at[2 + e])
    wait_bytes(whole_ints.at[pl.ds(0, 4)], sib_send)
    tab_end()


def packed_ladder(amplitudes, integrals, tables, listing, occ_shift, virt_shift):
    dma = pltpu.SemaphoreType.DMA
    vmem, anywhere = pl.BlockSpec(memory_space=pltpu.VMEM), pl.BlockSpec(memory_space=pl.ANY)
    out, over, _, _ = pl.pallas_call(
        packed_kernel,
        name="packed_ladder",
        out_shape=(
            jax.ShapeDtypeStruct((8 * ROWS // TILE, TILE, 128), F32),
            jax.ShapeDtypeStruct((8, 128), jnp.int32),
            jax.ShapeDtypeStruct((2, 4, 4, PAIRS, TILE, 128), F32),
            jax.ShapeDtypeStruct((8, INT_PAIRS, TILE, 128), F32),
        ),
        in_specs=[vmem] * 3 + [pl.BlockSpec(memory_space=pltpu.SMEM)] + [vmem] * 2,
        out_specs=(anywhere, vmem, anywhere, anywhere),
        scratch_shapes=[
            pltpu.VMEM((2, PAIRS, TILE, 128), F32),
            pltpu.VMEM((INT_PAIRS, TILE, 128), F32),
            pltpu.VMEM((2, 4, 4, PAIRS, TILE, 128), F32),
            pltpu.VMEM((INT_PAIRS, TILE, 128), F32),
            pltpu.VMEM((INT_PAIRS, TILE, 128), F32),
            pltpu.VMEM((DEPTH, COLS), BF16),
            pltpu.VMEM((DEPTH, COLS), BF16),
            pltpu.VMEM((2 * CHUNK, DEPTH), BF16),
            pltpu.VMEM((2 * CHUNK, DEPTH), BF16),
            pltpu.VMEM((SLOTS, 4, CHUNK // TILE, TILE, 128), F32),
            pltpu.VMEM((4, 4, 8, 128), jnp.int32),
            pltpu.VMEM((4, 2, 8, 128), jnp.int32),
            pltpu.VMEM((4, 2, 8, 128), jnp.int32),
            pltpu.SMEM((4, 4, 8, 128), jnp.int32),
            pltpu.SMEM((4, 2, 8, 128), jnp.int32),
            dma((2, 4, 2)),
            dma((2, 4, 2, STEPS)),
            dma((4,)),
            dma((4, INT_PIECES)),
            dma,
            dma((4, INT_PIECES)),
            dma((14,)),
            dma((14,)),
            dma((SLOTS,)),
            dma((SLOTS,)),
            dma((8,)),
            dma((2,)),
            dma,
            dma((2,)),
            dma,
        ],
        compiler_params=pltpu.CompilerParams(collective_id=0, has_side_effects=True, vmem_limit_bytes=61 << 20),
        cost_estimate=pl.CostEstimate(flops=6 * ROWS * DEPTH * COLS, bytes_accessed=80 << 20, transcendentals=0),
    )(
        amplitudes.reshape(ROWS // TILE, TILE, 256), integrals, tables, listing, occ_shift.reshape(CHUNKS, 128),
        virt_shift.reshape(8, 128),
    )
    return out.reshape(8 * ROWS, 128), over[5, 0]


def shards(amplitudes, integrals, amp_mask, int_mask, occ_shift, virt_shift):
    halves = int_mask.reshape(8, 4, 2, 2).transpose(2, 0, 1, 3)
    masks = jnp.stack([amp_mask.reshape(128), halves.reshape(128)])
    count = jnp.arange(128, dtype=jnp.int32)
    slots = jnp.sum(jnp.where(count[:, None] < count[None, :], masks[:, :, None], 0), axis=1)
    used = slots + masks
    room = jnp.array([STEP_TILES * n for n in NEED], jnp.int32)
    over = jnp.any(used[0].reshape(CHUNKS, 8)[:, 7] > room) | (used[1, 63] > 2 * INT_EARLY * INT_PIECE) | (used[1, 127] > INT_MOST)
    limit = jnp.array([[MOST - 1], [INT_MOST - 1]], jnp.int32)
    at = jnp.where(masks != 0, jnp.minimum(slots, limit), 0)
    kind = jnp.where(masks != 0, 1 + ((at ^ count[None, :]) & 1), 0)
    here = (masks[:, :, None] != 0) & (slots[:, :, None] == count[None, None, :])
    place = jnp.sum(jnp.where(here, count[None, :, None], 0), axis=1)
    turn = 1 + ((place ^ count[None, :]) & 1)
    flags = jnp.broadcast_to(over.astype(jnp.int32), (128,))
    tables = jnp.stack([(at[0] >> 1) & 1, at[0] >> 2, kind[0], at[1] >> 1, kind[1], flags, flags, flags])
    a, b = place
    listing = jnp.stack([
        a >> 2, 1 - ((a >> 1) & 1), (a >> 1) & 1, turn[0], (b >> 3) & 7, (b >> 1) & 3, b >> 6, turn[1]
    ])
    update, over = packed_ladder(amplitudes, integrals, tables, listing, occ_shift, virt_shift)
    return lax.cond(
        over > 0,
        lambda: whole_ladder(amplitudes, integrals, amp_mask, int_mask, occ_shift, virt_shift),
        lambda: update,
    )


def solution(mesh):
    placed = (
        P("row", "col"),
        P("row", "col"),
        P("row", "col"),
        P("row", "col"),
        P("row"),
        P("col"),
    )
    return jax.shard_map(
        shards, mesh=mesh, in_specs=placed, out_specs=P(None, ("col", "row")), check_vma=False
    )
```

```python
import functools

import jax
import jax.numpy as jnp
from jax import lax
from jax.experimental import pallas as pl
from jax.experimental.pallas import tpu as pltpu
from jax.sharding import PartitionSpec as P

MESH = pl.DeviceIdType.MESH
F32, BF16 = jnp.float32, jnp.bfloat16
TILE = 64
ROWS, DEPTH, COLS = 2048, 4096, 1024
CHUNK = 128
CHUNKS = ROWS // CHUNK
HALF = CHUNK // 2
PIECE = 64
PIECES = 512 // PIECE
AHEAD = 5
CATCH = 2 * AHEAD
WIDE = 512


def wait_bytes(ref, sem):
    pltpu.make_async_copy(ref, ref, sem).wait()


def whole_kernel(
    amps, ints, amp_gain, int_gain, occ, virt,
    out, whole_amps,
    own, whole_ints, high, low, chunk_in, split, stage,
    amp_send, amp_recv, int_send, int_recv, sib_send, sib_recv, out_send, out_recv, local, load,
):
    row, col = lax.axis_index("row"), lax.axis_index("col")
    y, core = row // 2, row % 2
    z, x = col // 4, col % 4

    def at(dy=0, dz=0, dx=0, dcore=0):
        r = lax.rem(y + dy, 4) * 2 + lax.rem(core + dcore, 2)
        return r, lax.rem(z + dz, 4) * 4 + lax.rem(x + dx, 4)

    sibling = at(dcore=1)
    y_next, y_prev = at(dy=1), at(dy=3)
    x_near = (at(dx=1), at(dx=3))
    z_near = (at(dz=1), at(dz=3))
    first, second = (x_near, z_near), (z_near, x_near)
    partners = [*x_near, *z_near, sibling] + [at(dy=d, dcore=c) for d in (1, 2, 3) for c in (0, 1)]

    barrier = pltpu.get_barrier_semaphore()
    for partner in partners:
        pl.semaphore_signal(barrier, inc=1, device_id=partner, device_id_type=MESH)
    pl.semaphore_wait(barrier, len(partners))

    def remote(src, dst, send, recv, device):
        pltpu.make_async_remote_copy(
            src_ref=src, dst_ref=dst, send_sem=send, recv_sem=recv, device_id=device, device_id_type=MESH
        ).start()

    def rows_of(c, part=None):
        if part is None:
            return pl.ds(pl.multiple_of(c * CHUNK, CHUNK), CHUNK)
        return pl.ds(pl.multiple_of(c * CHUNK + part * HALF, HALF), HALF)

    def block(way, dz, dx, rows):
        return whole_amps.at[way, lax.rem(z + dz, 4), lax.rem(x + dx, 4), rows, :]

    def bundle(way, d, rows):
        if way == 0:
            return whole_amps.at[0, lax.rem(z + d, 4), :, rows, :]
        return whole_amps.at[1, :, lax.rem(x + d, 4), rows, :]

    def near(way, d, rows):
        return block(way, 0, d, rows) if way == 0 else block(way, d, 0, rows)

    def step1(c):
        rows = rows_of(c)
        for way in (0, 1):
            for e in (0, 1):
                remote(own.at[way, rows, :], block(way, 0, 0, rows), amp_send.at[way, 0, e], amp_recv.at[way, 0, e, c], first[way][e])

    def step2(c):
        for way in (0, 1):
            for e in (0, 1):
                d = 3 if e == 0 else 1
                wait_bytes(near(way, d, rows_of(c)), amp_recv.at[way, 0, e, c])
                part = near(way, d, rows_of(c, e))
                remote(part, part, amp_send.at[way, 1, e], amp_recv.at[way, 1, e, c], first[way][e])

    def step3(c):
        for way in (0, 1):
            for e in (0, 1):
                wait_bytes(near(way, 2, rows_of(c, e)), amp_recv.at[way, 1, e, c])
            line = bundle(way, 0, rows_of(c))
            for e in (0, 1):
                remote(line, line, amp_send.at[way, 2, e], amp_recv.at[way, 2, e, c], second[way][e])

    def step4(c):
        for way in (0, 1):
            for e in (0, 1):
                d = 3 if e == 0 else 1
                wait_bytes(bundle(way, d, rows_of(c)), amp_recv.at[way, 2, e, c])
                part = bundle(way, d, rows_of(c, e))
                remote(part, part, amp_send.at[way, 3, e], amp_recv.at[way, 3, e, c], second[way][e])

    def step5(c):
        for way in (0, 1):
            for e in (0, 1):
                wait_bytes(bundle(way, 2, rows_of(c, e)), amp_recv.at[way, 3, e, c])

    def tick(t):
        for lead, step in ((4, step1), (3, step2), (2, step3), (1, step4), (0, step5)):
            c = t + lead
            pl.when((c >= (4 if lead == 4 else 0)) & (c < CHUNKS))(functools.partial(step, c))

    def int_rows(p, part=None):
        if part is None:
            return pl.ds(pl.multiple_of(p * PIECE, PIECE), PIECE)
        return pl.ds(pl.multiple_of(p * PIECE + part * (PIECE // 2), PIECE // 2), PIECE // 2)

    def int_block(dy, dcore, rows):
        return whole_ints.at[lax.rem(y + dy, 4) * 2 + lax.rem(core + dcore, 2), rows, :]

    def halve(dy, dcore, rows_at, count):
        b = lax.rem(y + dy, 4) * 2 + lax.rem(core + dcore, 2)
        value = whole_ints[b, pl.ds(rows_at, count), :]
        top = value.astype(BF16)
        rows = pl.ds(pl.multiple_of(b * 512 + rows_at, count), count)
        high[rows, :] = top
        low[rows, :] = (value - top.astype(F32)).astype(BF16)

    def int_start(p):
        rows = int_rows(p)
        piece = int_block(0, 0, rows)
        remote(piece, piece, int_send.at[0], int_recv.at[0, p], y_next)
        remote(piece, piece, int_send.at[1], int_recv.at[1, p], y_prev)
        remote(piece, piece, sib_send, sib_recv.at[0, p], sibling)

    def int_pass(p):
        rows = int_rows(p)
        for e, d, device in ((0, 3, y_next), (1, 1, y_prev)):
            piece = int_block(d, 0, rows)
            wait_bytes(piece, int_recv.at[e, p])
            part = int_block(d, 0, int_rows(p, e))
            remote(part, part, int_send.at[2 + e], int_recv.at[2 + e, p], device)
            remote(piece, piece, sib_send, sib_recv.at[1 + e, p], sibling)

    def int_near(p):
        base = pl.multiple_of(p * PIECE, PIECE)
        halve(0, 0, base, PIECE)
        halve(3, 0, base, PIECE)
        halve(1, 0, base, PIECE)

    def int_sibling(p):
        rows, base = int_rows(p), pl.multiple_of(p * PIECE, PIECE)
        for k, d in ((0, 0), (1, 3), (2, 1)):
            wait_bytes(int_block(d, 1, rows), sib_recv.at[k, p])
            halve(d, 1, base, PIECE)

    def int_far(p):
        rows, base = int_rows(p), pl.multiple_of(p * PIECE, PIECE)
        for e in (0, 1):
            wait_bytes(int_block(2, 0, int_rows(p, e)), int_recv.at[2 + e, p])
        piece = int_block(2, 0, rows)
        remote(piece, piece, sib_send, sib_recv.at[3, p], sibling)
        halve(2, 0, base, PIECE)

    def int_far_sibling(p):
        wait_bytes(int_block(2, 1, int_rows(p)), sib_recv.at[3, p])
        halve(2, 1, pl.multiple_of(p * PIECE, PIECE), PIECE)

    def mask_chunk(c):
        for k in range(CHUNK // TILE):
            rows = pl.ds(pl.multiple_of(c * CHUNK + k * TILE, TILE), TILE)
            gain = amp_gain[pl.ds(c * (CHUNK // TILE) + k, 1), :]
            value = amps[rows, :] * gain
            own[0, rows, :] = value[:, :128]
            own[1, rows, :] = value[:, 128:]

    for c in range(4):
        mask_chunk(c)
        step1(c)

    @pl.loop(0, PIECES)
    def _(p):
        rows = int_rows(p)
        whole_ints[row, rows, :] = ints[rows, :] * int_gain[pl.ds(p, 1), :]
        int_start(p)

    @pl.loop(4, CHUNKS)
    def _(c):
        mask_chunk(c)

    for way in (0, 1):
        pltpu.make_async_copy(own.at[way], whole_amps.at[way, z, x], local.at[way]).start()
    for way in (0, 1):
        pltpu.make_async_copy(own.at[way], whole_amps.at[way, z, x], local.at[way]).wait()

    @pl.loop(0, 3)
    def _(t):
        tick(t - 3)

    @pl.loop(0, AHEAD - 1)
    def _(t):
        tick(t)
        for q in (0, 1):
            int_pass(2 * t + q)
        for q in (0, 1):
            int_near(2 * t + q)

        @pl.when(t > 0)
        def _():
            for q in (0, 1):
                int_sibling(2 * t - 2 + q)

    tick(AHEAD - 1)
    for q in (0, 1):
        int_sibling(2 * (AHEAD - 2) + q)

    @pl.loop(0, PIECES // 2)
    def _(p):
        int_far(p)

    tick(AHEAD)

    @pl.loop(PIECES // 2, PIECES)
    def _(p):
        int_far(p)
        int_far_sibling(p - PIECES // 2)

    @pl.loop(PIECES // 2, PIECES)
    def _(p):
        int_far_sibling(p)

    def fetch(c):
        slot = lax.rem(c, 2)
        return pltpu.make_async_copy(whole_amps.at[:, :, :, rows_of(c), :], chunk_in.at[slot], load.at[slot])

    @pl.loop(0, CHUNKS)
    def _(c):
        @pl.when((c > 0) & ((c >= CATCH) | (lax.rem(c, 2) == 0)))
        def _():
            tick(jnp.where(c < CATCH, AHEAD + c // 2, c))

        @pl.when((c == 0) | (c >= CATCH))
        def _():
            fetch(c).start()

        fetch(c).wait()

        @pl.when(c < CATCH - 1)
        def _():
            fetch(c + 1).start()

        slot = lax.rem(c, 2)

        @pl.loop(0, 16)
        def _(k):
            value = jnp.concatenate([chunk_in[slot, 0, k // 4, lax.rem(k, 4)], chunk_in[slot, 1, k // 4, lax.rem(k, 4)]], axis=1)
            top = value.astype(BF16)
            at_k = pl.ds(pl.multiple_of(k * 256, 256), 256)
            split[pl.ds(0, CHUNK), at_k] = top
            split[pl.ds(CHUNK, CHUNK), at_k] = (value - top.astype(F32)).astype(BF16)

        rows = rows_of(c)

        @pl.loop(0, COLS // WIDE)
        def _(n):
            wide = pl.ds(pl.multiple_of(n * WIDE, WIDE), WIDE)
            both = jnp.dot(split[...], high[:, wide], preferred_element_type=F32)
            rest = jnp.dot(split[pl.ds(0, CHUNK)], low[:, wide], preferred_element_type=F32)
            scaled = (both[:CHUNK] + (both[CHUNK:] + rest)) / (occ[rows, :] + virt[:, wide])
            for q in range(WIDE // 128):
                stage[n * (WIDE // 128) + q, rows, :] = scaled[:, q * 128:(q + 1) * 128]

        there = pl.ds(pl.multiple_of(row * ROWS + c * CHUNK, CHUNK), CHUNK)
        for d in (4, 5, 2, 3, 6, 7, 1):
            owner = lax.rem(row + d, 8)
            remote(stage.at[owner, rows, :], out.at[there, :], out_send, out_recv.at[row], (owner, col))
        pltpu.make_async_copy(stage.at[row, rows, :], out.at[there, :], out_recv.at[row]).start()

    for source in range(8):
        wait_bytes(out.at[pl.ds(source * ROWS, ROWS), :], out_recv.at[source])
    wait_bytes(stage.at[pl.ds(0, 7)], out_send)
    for way in (0, 1):
        for e in (0, 1):
            wait_bytes(whole_amps.at[way, 0, 0], amp_send.at[way, 0, e])
            wait_bytes(whole_amps.at[way, 0, 0, pl.ds(0, ROWS // 2)], amp_send.at[way, 1, e])
            wait_bytes(whole_amps.at[way, 0], amp_send.at[way, 2, e])
            wait_bytes(whole_amps.at[way, 0, pl.ds(0, 2)], amp_send.at[way, 3, e])
    for e in (0, 1):
        wait_bytes(whole_ints.at[0], int_send.at[e])
        wait_bytes(whole_ints.at[0, pl.ds(0, 256)], int_send.at[2 + e])
    wait_bytes(whole_ints.at[pl.ds(0, 4)], sib_send)


def whole_ladder(amplitudes, integrals, amp_mask, int_mask, occ_shift, virt_shift):
    amp_gain = jnp.repeat(amp_mask.astype(F32), TILE, axis=1)
    int_gain = jnp.repeat(int_mask.astype(F32), TILE, axis=1)
    dma = pltpu.SemaphoreType.DMA
    vmem, anywhere = pl.BlockSpec(memory_space=pltpu.VMEM), pl.BlockSpec(memory_space=pl.ANY)
    out, _ = pl.pallas_call(
        whole_kernel,
        name="whole_ladder",
        out_shape=(
            jax.ShapeDtypeStruct((8 * ROWS, 128), F32),
            jax.ShapeDtypeStruct((2, 4, 4, ROWS, 128), F32),
        ),
        in_specs=[vmem] * 6,
        out_specs=(anywhere, anywhere),
        scratch_shapes=[
            pltpu.VMEM((2, ROWS, 128), F32),
            pltpu.VMEM((8, 512, COLS), F32),
            pltpu.VMEM((DEPTH, COLS), BF16),
            pltpu.VMEM((DEPTH, COLS), BF16),
            pltpu.VMEM((2, 2, 4, 4, CHUNK, 128), F32),
            pltpu.VMEM((2 * CHUNK, DEPTH), BF16),
            pltpu.VMEM((8, ROWS, 128), F32),
            dma((2, 4, 2)),
            dma((2, 4, 2, CHUNKS)),
            dma((4,)),
            dma((4, PIECES)),
            dma,
            dma((4, PIECES)),
            dma,
            dma((8,)),
            dma((2,)),
            dma((2,)),
        ],
        compiler_params=pltpu.CompilerParams(collective_id=1, has_side_effects=True, vmem_limit_bytes=60 << 20),
        cost_estimate=pl.CostEstimate(flops=6 * ROWS * DEPTH * COLS, bytes_accessed=80 << 20, transcendentals=0),
    )(amplitudes, integrals, amp_gain, int_gain, occ_shift[:, None], virt_shift[None, :])
    return out


MOST = 104
PAIRS = MOST // 4
STEPS = 13
STEP = PAIRS // STEPS
STEP_TILES = MOST // STEPS
NEED = (1, 2, 3, 4, 5, 6, 7, 7, 8, 9, 9, 10, 11, 12, 12, 13)
INT_MOST = 104
INT_PAIRS = INT_MOST // 2
INT_PIECES = 13
INT_PIECE = INT_PAIRS // INT_PIECES
INT_EARLY = 7
SLOTS = 8
EARLY = 4


def packed_kernel(
    amps, ints, tables, listing, occ, virt,
    out, over, whole_amps, whole_ints,
    own, own_ints, packed, int_a, int_b, high, low, split_a, split_b, stage, plane, ring, flags, plane_s, ring_s,
    amp_send, amp_recv, int_send, int_recv, sib_send, sib_recv, tab_send, tab_recv, out_send, out_self, out_recv, local, load,
    int_load, tab_load,
):
    row, col = lax.axis_index("row"), lax.axis_index("col")
    y, core = row // 2, row % 2
    z, x = col // 4, col % 4

    def at(dy=0, dz=0, dx=0, dcore=0):
        r = lax.rem(y + dy, 4) * 2 + lax.rem(core + dcore, 2)
        return r, lax.rem(z + dz, 4) * 4 + lax.rem(x + dx, 4)

    sibling = at(dcore=1)
    y_next, y_prev = at(dy=1), at(dy=3)
    x_near = (at(dx=1), at(dx=3))
    z_near = (at(dz=1), at(dz=3))
    first, second = (x_near, z_near), (z_near, x_near)
    partners = [*x_near, *z_near, sibling] + [at(dy=d, dcore=c) for d in (1, 2, 3) for c in (0, 1)]

    barrier = pltpu.get_barrier_semaphore()
    for partner in partners:
        pl.semaphore_signal(barrier, inc=1, device_id=partner, device_id_type=MESH)
    pl.semaphore_wait(barrier, len(partners))

    def remote(src, dst, send, recv, device):
        pltpu.make_async_remote_copy(
            src_ref=src, dst_ref=dst, send_sem=send, recv_sem=recv, device_id=device, device_id_type=MESH
        ).start()

    def plane_at(dz, dx):
        return plane.at[lax.rem(z + dz, 4), lax.rem(x + dx, 4)]

    def line_at(dz):
        return plane.at[lax.rem(z + dz, 4)]

    def ring_at(dy):
        return ring.at[lax.rem(y + dy, 4)]

    def tab(k, ref, device):
        remote(ref, ref, tab_send.at[k], tab_recv.at[k], device)

    def tab_wait(k, ref):
        wait_bytes(ref, tab_recv.at[k])

    def ring0():
        ring[y, core] = tables[...]
        tab(6, ring.at[y, core], sibling)

    def ring1():
        tab_wait(6, ring.at[y, 1 - core])
        tab(7, ring_at(0), y_next)
        tab(8, ring_at(0), y_prev)

    def ring2():
        tab_wait(7, ring_at(3))
        tab(9, ring_at(3), y_next)
        tab_wait(8, ring_at(1))

    def ring3():
        tab_wait(9, ring_at(2))
        pltpu.make_async_copy(ring, ring_s, tab_load).start()
        pltpu.make_async_copy(ring, ring_s, tab_load).wait()

    def plane0():
        plane[z, x] = tables[...]
        tab(0, plane_at(0, 0), x_near[0])
        tab(1, plane_at(0, 0), x_near[1])

    def plane1():
        tab_wait(0, plane_at(0, 3))
        tab(2, plane_at(0, 3), x_near[0])
        tab_wait(1, plane_at(0, 1))

    def plane2():
        tab_wait(2, plane_at(0, 2))
        tab(3, line_at(0), z_near[0])
        tab(4, line_at(0), z_near[1])

    def plane3():
        tab_wait(3, line_at(3))
        tab(5, line_at(3), z_near[0])
        tab_wait(4, line_at(1))

    def plane4():
        tab_wait(5, line_at(2))
        pltpu.make_async_copy(plane, plane_s, tab_load).start()
        pltpu.make_async_copy(plane, plane_s, tab_load).wait()

    def flag0():
        most = jnp.zeros((8, 128), jnp.int32)
        for zz in range(4):
            for xx in range(4):
                most = jnp.maximum(most, plane[zz, xx])
        flags[y, core] = most
        tab(10, flags.at[y, core], sibling)

    def flag1():
        tab_wait(10, flags.at[y, 1 - core])
        tab(11, flags.at[y], y_next)
        tab(12, flags.at[y], y_prev)

    def flag2():
        tab_wait(11, flags.at[lax.rem(y + 3, 4)])
        tab(13, flags.at[lax.rem(y + 3, 4)], y_next)
        tab_wait(12, flags.at[lax.rem(y + 1, 4)])

    def flag3():
        tab_wait(13, flags.at[lax.rem(y + 2, 4)])
        most = jnp.zeros((8, 128), jnp.int32)
        for yy in range(4):
            for cc in range(2):
                most = jnp.maximum(most, flags[yy, cc])
        over[...] = most

    def tab_end():
        for k, ref in enumerate((
            plane_at(0, 0), plane_at(0, 0), plane_at(0, 0), line_at(0), line_at(0), line_at(0), ring.at[0, 0], ring_at(0),
            ring_at(0), ring_at(0), flags.at[0, 0], flags.at[0], flags.at[0], flags.at[0],
        )):
            wait_bytes(ref, tab_send.at[k])

    lane = lax.broadcasted_iota(jnp.int32, (TILE, 128), 1)
    lane_row = lax.broadcasted_iota(jnp.int32, (1, 128), 1)

    def beside(left, right, left_kind, right_kind):
        kinds = jnp.where(lane_row < 64, left_kind, right_kind)
        straight = (kinds & 1).astype(F32)
        turned = (kinds >> 1).astype(F32)
        return (
            jnp.where(lane < 64, left, right) * straight
            + pltpu.roll(jnp.where(lane < 64, right, left), 64, 1) * turned
        )

    def rows_of(c, part=None):
        return pl.ds(c * STEP, STEP) if part is None else pl.ds(c * STEP + part, 1)

    def block(way, dz, dx, rows):
        return whole_amps.at[way, lax.rem(z + dz, 4), lax.rem(x + dx, 4), rows]

    def bundle(way, d, rows):
        if way == 0:
            return whole_amps.at[0, lax.rem(z + d, 4), :, rows]
        return whole_amps.at[1, :, lax.rem(x + d, 4), rows]

    def near(way, d, rows):
        return block(way, 0, d, rows) if way == 0 else block(way, d, 0, rows)

    def step1(c):
        rows = rows_of(c)
        for way in (0, 1):
            for e in (0, 1):
                remote(own.at[way, rows], block(way, 0, 0, rows), amp_send.at[way, 0, e], amp_recv.at[way, 0, e, c], first[way][e])

    def step2(c):
        for way in (0, 1):
            for e in (0, 1):
                d = 3 if e == 0 else 1
                wait_bytes(near(way, d, rows_of(c)), amp_recv.at[way, 0, e, c])
                part = near(way, d, rows_of(c, e))
                remote(part, part, amp_send.at[way, 1, e], amp_recv.at[way, 1, e, c], first[way][e])

    def step3(c):
        for way in (0, 1):
            for e in (0, 1):
                wait_bytes(near(way, 2, rows_of(c, e)), amp_recv.at[way, 1, e, c])
            line = bundle(way, 0, rows_of(c))
            for e in (0, 1):
                remote(line, line, amp_send.at[way, 2, e], amp_recv.at[way, 2, e, c], second[way][e])

    def step4(c):
        for way in (0, 1):
            for e in (0, 1):
                d = 3 if e == 0 else 1
                wait_bytes(bundle(way, d, rows_of(c)), amp_recv.at[way, 2, e, c])
                part = bundle(way, d, rows_of(c, e))
                remote(part, part, amp_send.at[way, 3, e], amp_recv.at[way, 3, e, c], second[way][e])

    def step5(c):
        for way in (0, 1):
            for e in (0, 1):
                wait_bytes(bundle(way, 2, rows_of(c, e)), amp_recv.at[way, 3, e, c])

    def tick(t, leads=(2, 4, 6, 8)):
        for lead, step in zip(leads, (step4, step3, step2, step1)):
            c = t + lead
            pl.when((c >= 0) & (c < STEPS))(functools.partial(step, c))

    def brisk(t):
        tick(t, (1, 2, 3, 5 if t >= 0 else STEPS + 3))

    def fetch(s):
        rows = rows_of(s)
        return pltpu.make_async_copy(whole_amps.at[:, :, :, rows], packed.at[:, :, :, rows], load)

    def arrive(s):
        step5(s)
        fetch(s).start()
        fetch(s).wait()

    def int_rows(p, part=None):
        half = INT_PIECE // 2
        return pl.ds(p * INT_PIECE, INT_PIECE) if part is None else pl.ds(p * INT_PIECE + part * half, half)

    def int_block(dy, dcore, rows):
        return whole_ints.at[lax.rem(y + dy, 4) * 2 + lax.rem(core + dcore, 2), rows]

    def unpack_ints(ref, dy, dcore, half):
        yy, cc = lax.rem(y + dy, 4), lax.rem(core + dcore, 2)

        @pl.loop(0, 8)
        def _(t):
            rows = pl.ds(pl.multiple_of((yy * 2 + cc) * 512 + t * TILE, TILE), TILE)
            for g in range(4):
                one = half * 64 + t * 8 + 2 * g
                two = one + 1
                value = beside(
                    ref[ring_s[yy, cc, 3, one]], ref[ring_s[yy, cc, 3, two]], ring_s[yy, cc, 4, one], ring_s[yy, cc, 4, two]
                )
                top = value.astype(BF16)
                lanes = slice((half * 4 + g) * 128, (half * 4 + g + 1) * 128)
                high[rows, lanes] = top
                low[rows, lanes] = (value - top.astype(F32)).astype(BF16)

    def int_start(p):
        rows = int_rows(p)
        piece, there = own_ints.at[rows], int_block(0, 0, rows)
        remote(piece, there, int_send.at[0], int_recv.at[0, p], y_next)
        remote(piece, there, int_send.at[1], int_recv.at[1, p], y_prev)

    def int_pass(p):
        rows = int_rows(p)
        for e, d, device in ((0, 3, y_next), (1, 1, y_prev)):
            piece = int_block(d, 0, rows)
            wait_bytes(piece, int_recv.at[e, p])
            part = int_block(d, 0, int_rows(p, e))
            remote(part, part, int_send.at[2 + e], int_recv.at[2 + e, p], device)
            remote(piece, piece, sib_send, sib_recv.at[1 + e, p], sibling)

    def int_take(blocks, half):
        first, last = ((0, INT_EARLY), (INT_EARLY, INT_PIECES))[half]

        def enter(i):
            k, dy, dcore = blocks[i]
            if dcore and k == 0:
                wait_bytes(int_block(0, 1, pl.ds(0, INT_PAIRS)), sib_recv.at[0, 0])
            elif dcore:
                @pl.loop(first, last)
                def _(p):
                    wait_bytes(int_block(dy, 1, int_rows(p)), sib_recv.at[k, p])
            pairs = pl.ds(0, INT_PAIRS if half or k == 0 else INT_EARLY * INT_PIECE)
            buffer = (int_a, int_b)[i % 2]
            copy = pltpu.make_async_copy(int_block(dy, dcore, pairs), buffer.at[pairs], int_load.at[i % 2])
            copy.start()
            return copy

        copy = enter(0)
        for i, (k, dy, dcore) in enumerate(blocks):
            copy.wait()
            copy = enter(i + 1) if i + 1 < len(blocks) else None
            unpack_ints((int_a, int_b)[i % 2], dy, dcore, half)
            if k == 0:
                unpack_ints((int_a, int_b)[i % 2], dy, dcore, 1)

    def int_far(p):
        for e in (0, 1):
            wait_bytes(int_block(2, 0, int_rows(p, e)), int_recv.at[2 + e, p])
        piece = int_block(2, 0, int_rows(p))
        remote(piece, piece, sib_send, sib_recv.at[3, p], sibling)

    ring0()
    plane0()

    @pl.loop(0, PAIRS)
    def _(i):
        for way in (0, 1):
            pair = 2 * i + way
            tiles = []
            for place in (2 * pair, 2 * pair + 1):
                both = amps[listing[0, place]]
                tiles.append(both[:, :128] * listing[1, place].astype(F32) + both[:, 128:] * listing[2, place].astype(F32))
            own[way, i] = beside(*tiles, listing[3, 2 * pair], listing[3, 2 * pair + 1])

    for c in range(5):
        step1(c)
    ring1()

    for t in range(8):
        for g in range(8):
            stage[t, g // 2, g % 2] = ints[t * TILE:(t + 1) * TILE, g * 128:(g + 1) * 128]

    @pl.loop(0, INT_PAIRS)
    def _(pair):
        one = 2 * pair
        two = one + 1
        own_ints[pair] = beside(
            stage[listing[4, one], listing[5, one], listing[6, one]], stage[listing[4, two], listing[5, two], listing[6, two]],
            listing[7, one], listing[7, two],
        )

    ring2()

    @pl.loop(0, INT_EARLY)
    def _(p):
        int_start(p)

    remote(own_ints, int_block(0, 0, pl.ds(0, INT_PAIRS)), sib_send, sib_recv.at[0, 0], sibling)
    for way in (0, 1):
        pltpu.make_async_copy(own.at[way], whole_amps.at[way, z, x], local.at[way]).start()
    for way in (0, 1):
        pltpu.make_async_copy(own.at[way], whole_amps.at[way, z, x], local.at[way]).wait()

    brisk(-3)
    plane1()
    ring3()
    unpack_ints(own_ints, 0, 0, 0)
    brisk(-2)
    plane2()
    unpack_ints(own_ints, 0, 0, 1)
    int_pass(0)
    int_pass(1)
    int_take([(0, 0, 1)], 0)
    brisk(-1)
    plane3()

    @pl.loop(2, INT_EARLY)
    def _(p):
        int_pass(p)

    @pl.loop(INT_EARLY, INT_PIECES)
    def _(p):
        int_start(p)

    brisk(0)
    plane4()
    flag0()
    int_take([(1, 3, 0), (2, 1, 0), (1, 3, 1), (2, 1, 1)], 0)

    @pl.loop(0, INT_EARLY)
    def _(p):
        int_far(p)

    brisk(1)
    flag1()
    int_take([(3, 2, 0), (3, 2, 1)], 0)
    arrive(0)
    arrive(1)

    @pl.loop(INT_EARLY, INT_EARLY + 2)
    def _(p):
        int_pass(p)

    step2(5)
    step1(7)
    step1(8)

    def stage_wait(slot):
        wait_bytes(stage.at[slot, pl.ds(0, 3)], out_send.at[slot])
        wait_bytes(stage.at[slot, 0], out_self.at[slot])

    def unpack_amps(split, c, zz, xx, at_k):
        for t in (0, 1):
            for g in (0, 1):
                one = (c * 2 + t) * 4 + 2 * g
                two = one + 1
                value = beside(
                    packed[plane_s[zz, xx, 0, one], zz, xx, plane_s[zz, xx, 1, one]],
                    packed[plane_s[zz, xx, 0, two], zz, xx, plane_s[zz, xx, 1, two]],
                    plane_s[zz, xx, 2, one], plane_s[zz, xx, 2, two],
                )
                top = value.astype(BF16)
                lanes = pl.ds(pl.multiple_of(at_k + g * 128, 128), 128)
                split[t * TILE:(t + 1) * TILE, lanes] = top
                split[CHUNK + t * TILE:CHUNK + (t + 1) * TILE, lanes] = (value - top.astype(F32)).astype(BF16)

    @pl.loop(0, 16)
    def _(k):
        unpack_amps(split_a, 0, k // 4, lax.rem(k, 4), k * 256)

    def multiply(unit, c, n, split, split_next, later, parts):
        slot = lax.rem(unit, SLOTS)
        pl.when(unit >= SLOTS)(functools.partial(stage_wait, slot))
        shift = jnp.transpose(jnp.broadcast_to(occ[pl.ds(c, 1), :], (CHUNK, 128)))
        wide = pl.ds(pl.multiple_of(n * WIDE, WIDE), WIDE)
        both = jnp.dot(split[...], high[:, wide], preferred_element_type=F32)
        for zz, xx, at_k in parts:
            unpack_amps(split_next, later, zz, xx, at_k)
        rest = jnp.dot(split[0:CHUNK], low[:, wide], preferred_element_type=F32)
        ladder = both[:CHUNK] + (both[CHUNK:] + rest)
        for q in range(4):
            scaled = ladder[:, q * 128:(q + 1) * 128] / (shift + virt[pl.ds(2 * q + n, 1), :])
            stage[slot, q, 0] = scaled[:TILE]
            stage[slot, q, 1] = scaled[TILE:]

        there = pl.ds(row * (ROWS // TILE) + c * (CHUNK // TILE), CHUNK // TILE)
        for d in (2, 1, 3):
            owner = lax.rem(y + d, 4)
            remote(stage.at[slot, owner], out.at[there], out_send.at[slot], out_recv.at[row], (owner * 2 + n, col))

        @pl.when(core == n)
        def _():
            pltpu.make_async_copy(stage.at[slot, y], out.at[there], out_self.at[slot]).start()

        @pl.when(core != n)
        def _():
            remote(stage.at[slot, y], out.at[there], out_self.at[slot], out_recv.at[row], sibling)

    def after(value, points):
        return sum((value >= p).astype(jnp.int32) for p in points)

    def among(value, points):
        return functools.reduce(lambda a, b: a | b, [value == p for p in points])

    @pl.loop(0, 16)
    def _(k):
        unpack_amps(split_a, 0, k // 4, lax.rem(k, 4), k * 256)

    everything = [(k // 4, k % 4, k * 256) for k in range(16)]

    @pl.loop(0, EARLY)
    def _(i):
        for odd, split, split_next in ((0, split_a, split_b), (1, split_b, split_a)):
            unit = 2 * i + odd
            n = unit // EARLY
            c = unit - n * EARLY

            @pl.when(among(unit, (1, 2, 4, 6)))
            def _():
                tick(1 + after(unit, (2, 4, 6)))

            @pl.when(among(unit, (1, 2, 5, 7)))
            def _():
                arrive(2 + after(unit, (2, 5, 7)))

            later = jnp.where((unit == EARLY - 1), 0, c + 1)
            multiply(unit, c, n, split, split_next, later, everything)
            if odd == 0:
                @pl.when(i == 0)
                def _():
                    int_pass(INT_EARLY + 2)
                    int_pass(INT_EARLY + 3)
                    step3(4)
                    step2(6)
            else:
                @pl.when(i == 0)
                def _():
                    int_pass(INT_EARLY + 4)
                    int_pass(INT_EARLY + 5)
                    flag2()
                    int_take([(1, 3, 0), (2, 1, 0), (1, 3, 1), (2, 1, 1)], 1)

                @pl.when(i == 1)
                def _():
                    @pl.loop(INT_EARLY, INT_PIECES)
                    def _(p):
                        int_far(p)

                    int_take([(3, 2, 0), (3, 2, 1)], 1)

    @pl.loop(EARLY // 2, CHUNKS // 2)
    def _(i):
        for odd, split, split_next in ((0, split_a, split_b), (1, split_b, split_a)):
            c = 2 * i + odd

            @pl.when(among(c, (5, 6, 8, 10, 11, 13)))
            def _():
                tick(5 + after(c, (6, 8, 10, 11, 13)))

            later = jnp.minimum(c + 1, CHUNKS - 1)
            multiply(2 * c, c, 0, split, split_next, later, [])

            @pl.when(among(c, (5, 7, 8, 10, 11, 12, 14)))
            def _():
                arrive(6 + after(c, (7, 8, 10, 11, 12, 14)))

            multiply(2 * c + 1, c, 1, split, split_next, later, everything)

    flag3()
    for slot in range(SLOTS):
        stage_wait(slot)
    for d in range(1, 8):
        source = lax.rem(row + d, 8)
        wait_bytes(out.at[pl.ds(source * (ROWS // TILE), ROWS // TILE)], out_recv.at[source])
    for way in (0, 1):
        for e in (0, 1):
            wait_bytes(whole_amps.at[way, 0, 0], amp_send.at[way, 0, e])
            wait_bytes(whole_amps.at[way, 0, 0, pl.ds(0, PAIRS // 2)], amp_send.at[way, 1, e])
            wait_bytes(whole_amps.at[way, 0], amp_send.at[way, 2, e])
            wait_bytes(whole_amps.at[way, 0, pl.ds(0, 2)], amp_send.at[way, 3, e])
    for e in (0, 1):
        wait_bytes(whole_ints.at[0], int_send.at[e])
        wait_bytes(whole_ints.at[0, pl.ds(0, INT_PAIRS // 2)], int_send.at[2 + e])
    wait_bytes(whole_ints.at[pl.ds(0, 4)], sib_send)
    tab_end()


def packed_ladder(amplitudes, integrals, tables, listing, occ_shift, virt_shift):
    dma = pltpu.SemaphoreType.DMA
    vmem, anywhere = pl.BlockSpec(memory_space=pltpu.VMEM), pl.BlockSpec(memory_space=pl.ANY)
    out, over, _, _ = pl.pallas_call(
        packed_kernel,
        name="packed_ladder",
        out_shape=(
            jax.ShapeDtypeStruct((8 * ROWS // TILE, TILE, 128), F32),
            jax.ShapeDtypeStruct((8, 128), jnp.int32),
            jax.ShapeDtypeStruct((2, 4, 4, PAIRS, TILE, 128), F32),
            jax.ShapeDtypeStruct((8, INT_PAIRS, TILE, 128), F32),
        ),
        in_specs=[vmem] * 3 + [pl.BlockSpec(memory_space=pltpu.SMEM)] + [vmem] * 2,
        out_specs=(anywhere, vmem, anywhere, anywhere),
        scratch_shapes=[
            pltpu.VMEM((2, PAIRS, TILE, 128), F32),
            pltpu.VMEM((INT_PAIRS, TILE, 128), F32),
            pltpu.VMEM((2, 4, 4, PAIRS, TILE, 128), F32),
            pltpu.VMEM((INT_PAIRS, TILE, 128), F32),
            pltpu.VMEM((INT_PAIRS, TILE, 128), F32),
            pltpu.VMEM((DEPTH, COLS), BF16),
            pltpu.VMEM((DEPTH, COLS), BF16),
            pltpu.VMEM((2 * CHUNK, DEPTH), BF16),
            pltpu.VMEM((2 * CHUNK, DEPTH), BF16),
            pltpu.VMEM((SLOTS, 4, CHUNK // TILE, TILE, 128), F32),
            pltpu.VMEM((4, 4, 8, 128), jnp.int32),
            pltpu.VMEM((4, 2, 8, 128), jnp.int32),
            pltpu.VMEM((4, 2, 8, 128), jnp.int32),
            pltpu.SMEM((4, 4, 8, 128), jnp.int32),
            pltpu.SMEM((4, 2, 8, 128), jnp.int32),
            dma((2, 4, 2)),
            dma((2, 4, 2, STEPS)),
            dma((4,)),
            dma((4, INT_PIECES)),
            dma,
            dma((4, INT_PIECES)),
            dma((14,)),
            dma((14,)),
            dma((SLOTS,)),
            dma((SLOTS,)),
            dma((8,)),
            dma((2,)),
            dma,
            dma((2,)),
            dma,
        ],
        compiler_params=pltpu.CompilerParams(collective_id=0, has_side_effects=True, vmem_limit_bytes=61 << 20),
        cost_estimate=pl.CostEstimate(flops=6 * ROWS * DEPTH * COLS, bytes_accessed=80 << 20, transcendentals=0),
    )(
        amplitudes.reshape(ROWS // TILE, TILE, 256), integrals, tables, listing, occ_shift.reshape(CHUNKS, 128),
        virt_shift.reshape(8, 128),
    )
    return out.reshape(8 * ROWS, 128), over[5, 0]


def shards(amplitudes, integrals, amp_mask, int_mask, occ_shift, virt_shift):
    halves = int_mask.reshape(8, 4, 2, 2).transpose(2, 0, 1, 3)
    masks = jnp.stack([amp_mask.reshape(128), halves.reshape(128)])
    count = jnp.arange(128, dtype=jnp.int32)
    slots = jnp.sum(jnp.where(count[:, None] < count[None, :], masks[:, :, None], 0), axis=1)
    used = slots + masks
    room = jnp.array([STEP_TILES * n for n in NEED], jnp.int32)
    over = jnp.any(used[0].reshape(CHUNKS, 8)[:, 7] > room) | (used[1, 63] > 2 * INT_EARLY * INT_PIECE) | (used[1, 127] > INT_MOST)
    limit = jnp.array([[MOST - 1], [INT_MOST - 1]], jnp.int32)
    at = jnp.where(masks != 0, jnp.minimum(slots, limit), 0)
    kind = jnp.where(masks != 0, 1 + ((at ^ count[None, :]) & 1), 0)
    here = (masks[:, :, None] != 0) & (slots[:, :, None] == count[None, None, :])
    place = jnp.sum(jnp.where(here, count[None, :, None], 0), axis=1)
    turn = 1 + ((place ^ count[None, :]) & 1)
    flags = jnp.broadcast_to(over.astype(jnp.int32), (128,))
    tables = jnp.stack([(at[0] >> 1) & 1, at[0] >> 2, kind[0], at[1] >> 1, kind[1], flags, flags, flags])
    a, b = place
    listing = jnp.stack([
        a >> 2, 1 - ((a >> 1) & 1), (a >> 1) & 1, turn[0], (b >> 3) & 7, (b >> 1) & 3, b >> 6, turn[1]
    ])
    update, over = packed_ladder(amplitudes, integrals, tables, listing, occ_shift, virt_shift)
    return lax.cond(
        over > 0,
        lambda: whole_ladder(amplitudes, integrals, amp_mask, int_mask, occ_shift, virt_shift),
        lambda: update,
    )


def solution(mesh):
    placed = (
        P("row", "col"),
        P("row", "col"),
        P("row", "col"),
        P("row", "col"),
        P("row"),
        P("col"),
    )
    return jax.shard_map(
        shards, mesh=mesh, in_specs=placed, out_specs=P(None, ("col", "row")), check_vma=False
    )
```
